512 devices in a mesh: grp: 64 (over x, y, z_hi), tp: 8 (over z_lo, core).
Axes of the slice: x: 4, y: 4, z: 16 (z_hi: 4, z_lo: 4; z = z_hi * 4 + z_lo), core: 2. Of those that a mesh axis runs over, the one named last changes fastest.
Arguments:
- queries: bfloat16 [8192, 36864], P('grp', 'tp'), may hold values from -64 to 64
- trunk: bfloat16 [512, 576], P('grp'), may hold values from -4 to 4
- own: bfloat16 [8192, 576], P('grp'), may hold values from -6 to 6
- grad_out: bfloat16 [8192, 32768], P('grp', 'tp'), may hold values from -12 to 12
- visible: int32 [8192], P('grp'), may hold values from 2 to 512, as said below
Outputs:
- grad_query: bfloat16 [8192, 36864], P('grp', 'tp')
- grad_trunk: float32 [512, 576], P('grp')
- grad_own: float32 [8192, 576], P('grp')
The draws below stay inside these ranges and needn't reach their ends.
Inputs may be any that keep to these rules, and one draw needn't show every extreme that they name: `visible`: at least 2, so the first two trunk positions are always seen; the entry of token 0 is 512.
All inputs are finite; a program needn't handle non-finite values.
Results may differ from the reference program's by a relative error of at most 0.0048.
Values may be sent and summed in bfloat16 or wider, within the bound.
A program may use at most 64 MiB of HBM per device.

```python
import jax
import jax.numpy as jnp
from jax import lax

H = 64
HL = 512
HR = 64
HK = 576
QTOK = 8192
TRUNK = 512


def cache_keys(key):
    return jnp.clip(jax.random.normal(jax.random.fold_in(key, 77), (TRUNK, HK), jnp.float32), -4.0, 4.0)


def draw_trunk(key, part):
    base = cache_keys(key)
    return base.astype(jnp.bfloat16)


def draw_queries(key, part):
    key = jax.random.fold_in(key, 2)
    values = jnp.clip(jax.random.normal(key, (QTOK, H, HK), jnp.float32), -6.0, 6.0)
    return values.reshape(QTOK, H * HK).astype(jnp.bfloat16)


def draw_visible(key, part):
    key = jax.random.fold_in(key, 3)
    lengths = jax.random.randint(key, (QTOK,), 2, TRUNK + 1, jnp.int32)
    return lengths.at[0].set(TRUNK)


def steps_of(rng, extent, cuts, low, largest):
    loudness = 1.0
    for position, parts in cuts:
        heights = jax.random.uniform(jax.random.fold_in(jax.random.fold_in(rng, 6), position), (parts,), jnp.float32, low / len(cuts), largest / len(cuts))
        loudness = loudness * jnp.repeat(jnp.exp(heights), extent[position] // parts).reshape((-1,) + (1,) * (len(extent) - 1 - position))
    return loudness


def scatter_about(key, shape, deviation, limit, cuts=(), kind=jnp.bfloat16):
    result = jax.random.normal(key, shape, jnp.float32) * deviation
    if len(cuts) > 0:
        result = steps_of(key, shape, cuts, -0.22, 0.18) * result
    return jnp.clip(result, min=-limit, max=limit).astype(kind)


def setup_inputs(seed: int = 0) -> dict:
    key_list = jax.random.split(jax.random.key(seed), 6)
    return {
        "queries": draw_queries(jax.random.fold_in(key_list[5], 71), 0),
        "trunk": draw_trunk(jax.random.fold_in(key_list[5], 71), 0),
        "own": scatter_about(key_list[2], (QTOK, HK), 1.0, 6.0, ((0, 64),)),
        "grad_out": scatter_about(key_list[3], (QTOK, H * HL), 2.0, 12.0, ((0, 64), (1, 8))),
        "visible": draw_visible(jax.random.fold_in(key_list[5], 71), 0),
    }


score_scale = 192.0 ** -0.5


def head_grads(query, grad_head, trunk, own, mask):
    query_f = query.astype(jnp.float32)
    own_f = own.astype(jnp.float32)
    scores = jnp.dot(query, trunk.T, preferred_element_type=jnp.float32) * score_scale
    self_score = jnp.sum(query_f * own_f, axis=-1) * score_scale
    scores = jnp.where(mask, scores, jnp.float32(-1e30))
    top = jnp.maximum(jnp.max(scores, axis=-1), self_score)
    expo = jnp.where(mask, jnp.exp(scores - top[:, None]), jnp.float32(0.0))
    self_expo = jnp.exp(self_score - top)
    total = jnp.sum(expo, axis=-1) + self_expo
    prob = expo / total[:, None]
    self_prob = self_expo / total
    grad_f = grad_head.astype(jnp.float32)
    dprob = jnp.dot(grad_head, trunk[:, :HL].T, preferred_element_type=jnp.float32)
    self_dprob = jnp.sum(grad_f * own_f[:, :HL], axis=-1)
    delta = jnp.sum(prob * dprob, axis=-1) + self_prob * self_dprob
    dscore = prob * (dprob - delta[:, None])
    self_dscore = self_prob * (self_dprob - delta)
    prob_b = prob.astype(jnp.bfloat16)
    dscore_b = dscore.astype(jnp.bfloat16)
    grad_q = ((jnp.dot(dscore_b, trunk, preferred_element_type=jnp.float32) + self_dscore[:, None] * own_f) * score_scale).astype(jnp.bfloat16)
    value_grad = jnp.dot(prob_b.T, grad_head, preferred_element_type=jnp.float32)
    key_grad = jnp.dot(dscore_b.T, query, preferred_element_type=jnp.float32) * score_scale
    key_grad = key_grad + jnp.pad(value_grad, ((0, 0), (0, HR)))
    own_grad = self_dscore[:, None] * query_f * score_scale + jnp.pad(self_prob[:, None] * grad_f, ((0, 0), (0, HR)))
    return grad_q, key_grad, own_grad


def reference(queries, trunk, own, grad_out, visible):
    mask = jnp.arange(TRUNK, dtype=jnp.int32)[None, :] < visible[:, None]
    query_heads = queries.reshape(QTOK, H, HK).transpose(1, 0, 2)
    grad_heads = grad_out.reshape(QTOK, H, HL).transpose(1, 0, 2)

    def step(carry, pair):
        grad_q, key_grad, own_grad = head_grads(pair[0], pair[1], trunk, own, mask)
        return (carry[0] + key_grad, carry[1] + own_grad), grad_q

    start = (jnp.zeros((TRUNK, HK), jnp.float32), jnp.zeros((QTOK, HK), jnp.float32))
    (grad_trunk, grad_own), grad_q = lax.scan(step, start, (query_heads, grad_heads))
    grad_query = grad_q.transpose(1, 0, 2).reshape(QTOK, H * HK)
    return grad_query, grad_trunk, grad_own
```

```python
import jax
import jax.numpy as jnp
from jax import lax
from jax.experimental import pallas as pl
from jax.experimental.pallas import tpu as pltpu
from jax.sharding import PartitionSpec as P

HL = 512
HR = 64
HK = 576
KP = 640
HEADS = 8
TOK = 128
HALF = 320
MESH = pl.DeviceIdType.MESH
BF = jnp.bfloat16
F32 = jnp.float32

score_scale = 192.0 ** (-0.5)

PLANE = sorted(((dx, dy) for dx in range(4) for dy in range(4) if (dx, dy) != (0, 0)), key=lambda o: (-min(o[0], 4 - o[0]) - min(o[1], 4 - o[1]), o))
FAR_Z = sorted(range(1, 16), key=lambda k: (-min(k, 16 - k), k))


def rows16(start, size):
    return pl.ds(pl.multiple_of(start, 16), size)


def remote(src, dst, send, recv, where):
    return pltpu.make_async_remote_copy(
        src_ref=src, dst_ref=dst, send_sem=send, recv_sem=recv, device_id=where, device_id_type=MESH
    )


def pack(block):
    pad = jnp.zeros((8, 128), F32)
    tail = jnp.concatenate([block[:, 384:640], pad], axis=1)
    return jnp.concatenate([block[:, 0:384], tail], axis=0)


def unpack(block):
    return jnp.concatenate([block[0:8, :], block[8:16, 0:256]], axis=1)


def kernel(
    q_hbm, tr_hbm, own_hbm, g_hbm, vis_hbm,
    gq_hbm, gt_hbm, go_hbm,
    tr_ref, own_ref, vis_ref, gt_ref, got_ref,
    q_s, qo_s, g_s, k_s, bias_s, p_s, d_s, o_s,
    zg_src, zg_buf, kx_src, kx_buf, kacc, xr_src, xr_buf, zr_src, zr_buf, fin_src, fin_buf,
    os_src, oz_buf, ow_buf,
    lq, lo, lg, lw, ls, lf,
    zg_send, zg_recv, xg_send, xg_recv, cg_send, cg_recv, kx_send, kx_recv,
    xr_send, xr_recv, zr_send, zr_recv, fin_send, fin_recv, oz_send, oz_recv, og_send, og_recv, fo_send, fo_recv,
):
    g = lax.axis_index("grp")
    t = lax.axis_index("tp")
    xy, zh = g // 4, g % 4
    zl, core = t // 2, t % 2
    z = zh * 4 + zl
    other = 1 - core
    sib = (g, zl * 2 + other)

    def plane(n, sign):
        dx, dy = PLANE[n]
        return ((xy // 4 + 4 + sign * dx) % 4) * 4 + (xy % 4 + 4 + sign * dy) % 4

    def at_xy(n):
        return (plane(n, 1) * 4 + zh, t)

    def at_z(zz):
        return (xy * 4 + zz // 4, (zz % 4) * 2 + core)

    small = [
        pltpu.make_async_copy(src, dst, ls.at[i])
        for i, (src, dst) in enumerate([(tr_hbm, tr_ref), (own_hbm, own_ref), (vis_hbm, vis_ref)])
    ]
    for copy in small:
        copy.start()

    barrier = pltpu.get_barrier_semaphore()
    for k in FAR_Z:
        pl.semaphore_signal(barrier, inc=1, device_id=at_z((z + k) % 16), device_id_type=MESH)
    for n in range(15):
        pl.semaphore_signal(barrier, inc=1, device_id=at_xy(n), device_id_type=MESH)
    pl.semaphore_signal(barrier, inc=1, device_id=sib, device_id_type=MESH)

    def load_q(hp):
        return pltpu.make_async_copy(
            q_hbm.at[:, pl.ds(hp * 2 * HK, KP)], q_s.at[pl.ds(hp * 256, TOK)], lq.at[hp]
        )

    def load_o(hp):
        return pltpu.make_async_copy(
            q_hbm.at[:, pl.ds(hp * 2 * HK + HL, KP)], qo_s.at[pl.ds(hp * TOK, TOK)], lo.at[hp]
        )

    def load_g(h):
        return pltpu.make_async_copy(
            g_hbm.at[:, pl.ds(h * HL, HL)], g_s.at[pl.ds(h * TOK, TOK)], lg.at[h]
        )

    small[0].wait()
    slab = jnp.concatenate([tr_ref[...].astype(F32), jnp.zeros((8, KP - HK), F32)], axis=1)
    zg_src[...] = pack(slab).astype(BF)
    mine = (zh // 2) == core

    pl.semaphore_wait(barrier, 31)

    def zg(k):
        zz = (zh + k) % 4
        return remote(zg_src, zg_buf.at[zh], zg_send.at[k], zg_recv.at[zh], (xy * 4 + zz, t))

    def zg_from(src):
        return remote(zg_src, zg_buf.at[src], zg_send.at[0], zg_recv.at[src], (g, t))

    @pl.when(mine)
    def _():
        for k in range(1, 4):
            zg(k).start()
        zg_buf[zh] = zg_src[...]

    def zg_sent():
        @pl.when(mine)
        def _():
            for k in range(1, 4):
                zg(k).wait_send()

    drains = [zg_sent]

    for hp in range(HEADS // 2):
        load_q(hp).start()
        load_o(hp).start()
    for h in range(HEADS):
        load_g(h).start()
    small[1].wait()
    owns = own_ref[...].astype(F32).T.astype(BF)
    for cc in range(2):
        k_s[cc * HALF + 256 : (cc + 1) * HALF, :] = jnp.concatenate(
            [owns[cc * 64 : cc * 64 + 64, :], jnp.zeros((64, KP - HK), BF)], axis=1
        )
    small[2].wait()
    seen = vis_ref[...].reshape(1, TOK)
    low = jnp.float32(-1e30)
    for cc in range(2):
        row = lax.broadcasted_iota(jnp.int32, (256, TOK), 0)
        spot = (row // 16) * 32 + cc * 16 + row % 16
        bias_s[cc * HALF : cc * HALF + 256, :] = jnp.where(spot < seen, jnp.float32(0.0), low)
        row = lax.broadcasted_iota(jnp.int32, (64, TOK), 0) + cc * 64
        lane = lax.broadcasted_iota(jnp.int32, (64, TOK), 1)
        bias_s[cc * HALF + 256 : (cc + 1) * HALF, :] = jnp.where(row == lane, jnp.float32(0.0), low)

    for hp in range(HEADS // 2):
        load_q(hp).wait()
        load_o(hp).wait()
        odd = qo_s[hp * TOK : (hp + 1) * TOK, :].astype(F32)
        odd = jnp.concatenate([odd[:, 64:], odd[:, :64]], axis=1)
        q_s[hp * 256 + TOK : hp * 256 + 256, :] = odd.astype(BF)
    for h in range(HEADS):
        load_g(h).wait()

    for i in range(2):
        src = core * 2 + i

        @pl.when(src != zh)
        def _():
            zg_from(src).wait_recv()

    pair = jnp.concatenate([unpack(zg_buf[core * 2 + i].astype(F32)) for i in range(2)], axis=0)
    k_s[rows16(core * HALF + xy * 16, 16), :] = pair.astype(BF)

    def xg(k):
        block = k_s.at[rows16(core * HALF + xy * 16, 16)]
        return remote(block, block, xg_send.at[k], xg_recv.at[k], at_xy(k))

    def cg(n):
        spot = xy if n == 15 else plane(n, -1)
        block = k_s.at[rows16(core * HALF + spot * 16, 16)]
        return remote(block, block, cg_send.at[n], cg_recv.at[n], sib)

    def xg_got(n):
        block = k_s.at[rows16(core * HALF + plane(n, -1) * 16, 16)]
        return remote(block, block, xg_send.at[n], xg_recv.at[n], at_xy(n))

    def cg_got(n):
        spot = xy if n == 15 else plane(n, -1)
        block = k_s.at[rows16(other * HALF + spot * 16, 16)]
        return remote(block, block, cg_send.at[n], cg_recv.at[n], sib)

    for n in range(15):
        xg(n).start()
    cg(15).start()
    for n in reversed(range(15)):
        xg_got(n).wait_recv()
        cg(n).start()
    for n in reversed(range(16)):
        cg_got(n).wait_recv()

    def keys_sent():
        cg(15).wait_send()
        for n in range(15):
            xg(n).wait_send()
            cg(n).wait_send()

    drains.append(keys_sent)


    for hp in range(HEADS // 2):
        at = slice(hp * 256, hp * 256 + 256)
        nt = (((1,), (1,)), ((), ()))
        s = lax.dot_general(k_s[...], q_s[at, :], nt, preferred_element_type=F32)
        dp = lax.dot_general(k_s[:, 0:HL], g_s[at, :], nt, preferred_element_type=F32)
        bias = jnp.concatenate([bias_s[...], bias_s[...]], axis=1)
        s = s * score_scale + bias
        top = jnp.max(s, axis=0, keepdims=True)
        e = jnp.exp(s - top)
        inv = 1.0 / jnp.sum(e, axis=0, keepdims=True)
        p = e * inv
        delta = jnp.sum(p * dp, axis=0, keepdims=True)
        p_s[:, at] = p.astype(BF)
        d_s[:, at] = (p * (dp - delta)).astype(BF)

    def key_grad(half):
        at = rows16(half * HALF, HALF)
        a = jnp.dot(d_s[at, :], q_s[...], preferred_element_type=F32) * score_scale
        b = jnp.dot(p_s[at, :], g_s[...], preferred_element_type=F32)
        return jnp.concatenate([a[:, 0:HL] + b, a[:, HL:]], axis=1)

    kx_src[...] = key_grad(other).astype(BF)
    kx = remote(kx_src, kx_buf, kx_send, kx_recv, sib)
    kx.start()
    drains.append(kx.wait_send)
    kacc[...] = key_grad(core)
    kx.wait_recv()
    total = kacc[...] + kx_buf[...].astype(F32)
    kacc[...] = total
    xr_src[...] = total[0:256, :].astype(BF)
    os_src[...] = total[256:HALF, :].astype(BF)

    def xr(n):
        block = xr_src.at[rows16(plane(n, 1) * 16, 16)]
        return remote(block, xr_buf.at[n], xr_send.at[n], xr_recv.at[n], at_xy(n))

    for n in range(15):
        xr(n).start()

    def oz(k):
        to = (zl + k) % 4
        return remote(os_src.at[rows16(to * 16, 16)], oz_buf.at[zl], oz_send.at[k], oz_recv.at[zl], (g, to * 2 + core))

    def oz_from(k):
        src = (zl + k) % 4
        return remote(os_src.at[0:16], oz_buf.at[src], oz_send.at[k], oz_recv.at[src], (g, src * 2 + core))

    def og(k):
        block = ow_buf.at[rows16(core * 64 + zl * 16, 16)]
        return remote(block, block, og_send.at[k], og_recv.at[zl], (g, ((zl + k) % 4) * 2 + core))

    def og_from(k):
        src = (zl + k) % 4
        block = ow_buf.at[rows16(core * 64 + src * 16, 16)]
        return remote(block, block, og_send.at[k], og_recv.at[src], (g, src * 2 + core))

    for k in range(1, 4):
        oz(k).start()
    oz_buf[zl] = os_src[rows16(zl * 16, 16), :]

    def sums_sent():
        for n in range(15):
            xr(n).wait_send()
        for k in range(1, 4):
            oz(k).wait_send()

    drains.append(sums_sent)

    def store_q(hp):
        return pltpu.make_async_copy(
            o_s.at[:, pl.ds(pl.multiple_of(hp * 2 * HK, 128), 2 * HK)],
            gq_hbm.at[:, pl.ds(pl.multiple_of(hp * 2 * HK, 128), 2 * HK)],
            lw.at[hp],
        )

    @pl.loop(0, HEADS // 2)
    def _(hp):
        at = pl.ds(pl.multiple_of(hp * 256, 256), 256)
        tn = (((0,), (0,)), ((), ()))
        gq = lax.dot_general(d_s[:, at], k_s[...], tn, preferred_element_type=F32) * score_scale
        even, odd = gq[0:TOK, :], gq[TOK:, :]
        odd = jnp.concatenate([odd[:, HK:], odd[:, :HK]], axis=1)
        joint = jnp.concatenate([even[:, 0:HL], even[:, HL:] + odd[:, 0:128], odd[:, 128:]], axis=1)
        o_s[:, pl.ds(pl.multiple_of(hp * 2 * HK, 128), 2 * HK)] = joint.astype(BF)
        store_q(hp).start()

    drains.append(lambda: [store_q(hp).wait() for hp in range(HEADS // 2)])
    for k in range(1, 4):
        oz_from(k).wait_recv()
    own_sum = oz_buf[0].astype(F32)
    for a in range(1, 4):
        own_sum = own_sum + oz_buf[a].astype(F32)
    ow_buf[rows16(core * 64 + zl * 16, 16), :] = own_sum.astype(BF)
    for k in range(1, 4):
        og(k).start()
    drains.append(lambda: [og(k).wait_send() for k in range(1, 4)])

    total = kacc[rows16(xy * 16, 16), :]
    for n in reversed(range(15)):
        xr(n).wait_recv()
        total = total + xr_buf[n].astype(F32)
    zr_src[0] = pack(total[0:8, :]).astype(BF)
    zr_src[1] = pack(total[8:16, :]).astype(BF)

    def zr(i, a):
        to = (core * 2 + i) * 4 + a
        return remote(zr_src.at[i], zr_buf.at[z], zr_send.at[i * 4 + a], zr_recv.at[z], at_z(to))

    def zr_from(src):
        return remote(zr_src.at[0], zr_buf.at[src], zr_send.at[0], zr_recv.at[src], at_z(src))

    for i in range(2):
        for a in range(4):

            @pl.when((core * 2 + i) * 4 + a != z)
            def _():
                zr(i, a).start()

    def slabs_sent():
        for i in range(2):
            for a in range(4):

                @pl.when((core * 2 + i) * 4 + a != z)
                def _():
                    zr(i, a).wait_send()

    drains.append(slabs_sent)

    for k in range(1, 4):
        og_from(k).wait_recv()
    own_half = ow_buf.at[rows16(core * 64, 64)]
    fo = remote(own_half, own_half, fo_send, fo_recv, sib)
    fo.start()
    drains.append(fo.wait_send)
    own_half = ow_buf.at[rows16(other * 64, 64)]
    remote(own_half, own_half, fo_send, fo_recv, sib).wait_recv()
    got_ref[...] = ow_buf[...].astype(F32).T[0:HK, :]
    store_go = pltpu.make_async_copy(got_ref, go_hbm, lf.at[0])
    store_go.start()
    drains.append(store_go.wait)

    fin = remote(fin_src, fin_buf, fin_send, fin_recv, sib)

    @pl.when(mine)
    def _():
        zr_buf[z] = zr_src[zh % 2]
        total = jnp.zeros((16, 384), F32)
        for src in range(16):

            @pl.when(z != src)
            def _():
                zr_from(src).wait_recv()

            total = total + zr_buf[src].astype(F32)
        whole = unpack(total)
        fin_src[...] = whole
        fin.start()
        gt_ref[...] = whole[:, 0:HK]
        fin.wait_send()

    @pl.when(jnp.logical_not(mine))
    def _():
        fin.wait_recv()
        gt_ref[...] = fin_buf[:, 0:HK]

    store_gt = pltpu.make_async_copy(gt_ref, gt_hbm, lf.at[1])
    store_gt.start()
    drains.append(store_gt.wait)

    for drain in drains:
        drain()


def finish(q_in, t_in, o_in, q_out, t_out, o_out, q_s, t_s, o_s, sem, sem_out):
    pieces = [(q_in.at[pl.ds(i * 32, 32)], q_s.at[pl.ds(i * 32, 32)], q_out.at[pl.ds(i * 32, 32)]) for i in range(4)]
    pieces += [(o_in, o_s, o_out), (t_in, t_s, t_out)]
    loads = [pltpu.make_async_copy(p[0], p[1], sem.at[i]) for i, p in enumerate(pieces)]
    stores = [pltpu.make_async_copy(p[1], p[2], sem_out.at[i]) for i, p in enumerate(pieces)]
    for c in loads:
        c.start()
    for load, store in zip(loads, stores):
        load.wait()
        store.start()
    for c in stores:
        c.wait()


def per_device(queries, trunk, own, grad_out, visible):
    hbm = pl.BlockSpec(memory_space=pl.ANY)
    dma = pltpu.SemaphoreType.DMA
    grad_query, grad_trunk, grad_own = pl.pallas_call(
        kernel,
        out_shape=(
            jax.ShapeDtypeStruct((TOK, HEADS * HK), BF),
            jax.ShapeDtypeStruct((8, HK), F32),
            jax.ShapeDtypeStruct((HK, TOK), F32),
        ),
        in_specs=[hbm] * 5,
        out_specs=(hbm,) * 3,
        scratch_shapes=[
            pltpu.VMEM((8, HK), BF),
            pltpu.VMEM((HK, TOK), BF),
            pltpu.VMEM((TOK,), jnp.int32),
            pltpu.VMEM((8, HK), F32),
            pltpu.VMEM((HK, TOK), F32),
            pltpu.VMEM((HEADS * TOK, KP), BF),
            pltpu.VMEM((HEADS // 2 * TOK, KP), BF),
            pltpu.VMEM((HEADS * TOK, HL), BF),
            pltpu.VMEM((2 * HALF, KP), BF),
            pltpu.VMEM((2 * HALF, TOK), F32),
            pltpu.VMEM((2 * HALF, HEADS * TOK), BF),
            pltpu.VMEM((2 * HALF, HEADS * TOK), BF),
            pltpu.VMEM((TOK, HEADS * HK), BF),
            pltpu.VMEM((16, 384), BF),
            pltpu.VMEM((4, 16, 384), BF),
            pltpu.VMEM((HALF, KP), BF),
            pltpu.VMEM((HALF, KP), BF),
            pltpu.VMEM((HALF, KP), F32),
            pltpu.VMEM((256, KP), BF),
            pltpu.VMEM((16, 16, KP), BF),
            pltpu.VMEM((2, 16, 384), BF),
            pltpu.VMEM((16, 16, 384), BF),
            pltpu.VMEM((8, KP), F32),
            pltpu.VMEM((8, KP), F32),
            pltpu.VMEM((64, KP), BF),
            pltpu.VMEM((4, 16, KP), BF),
            pltpu.VMEM((TOK, KP), BF),
            dma((4,)), dma((4,)), dma((8,)), dma((4,)), dma((3,)), dma((2,)),
            dma((4,)), dma((4,)),
            dma((16,)), dma((16,)),
            dma((16,)), dma((16,)),
            dma, dma,
            dma((16,)), dma((16,)),
            dma((8,)), dma((16,)),
            dma, dma,
            dma((4,)), dma((4,)), dma((4,)), dma((4,)),
            dma, dma,
        ],
        compiler_params=pltpu.CompilerParams(
            collective_id=0, has_side_effects=True, vmem_limit_bytes=60 * 1024 * 1024
        ),
        cost_estimate=pl.CostEstimate(flops=3860000000, bytes_accessed=4500000, transcendentals=655360),
    )(queries, trunk, own.T, grad_out, visible)
    outs = [jax.ShapeDtypeStruct(a.shape, a.dtype) for a in (grad_query, grad_trunk, grad_own)]
    grad_query, grad_trunk, grad_own = pl.pallas_call(
        finish,
        out_shape=outs,
        in_specs=[hbm] * 3,
        out_specs=[hbm] * 3,
        scratch_shapes=[pltpu.VMEM(a.shape, a.dtype) for a in outs] + [dma((6,)), dma((6,))],
        compiler_params=pltpu.CompilerParams(vmem_limit_bytes=60 * 1024 * 1024),
    )(grad_query, grad_trunk, grad_own)
    return grad_query, grad_trunk, grad_own.T


def solution(mesh):
    in_specs = (P("grp", "tp"), P("grp", None), P("grp", None), P("grp", "tp"), P("grp"))
    out_specs = (P("grp", "tp"), P("grp", None), P("grp", None))
    return jax.shard_map(
        per_device, mesh=mesh, in_specs=in_specs, out_specs=out_specs, check_vma=False
    )
```

```python
import jax
import jax.numpy as jnp
from jax import lax
from jax.experimental import pallas as pl
from jax.experimental.pallas import tpu as pltpu
from jax.sharding import PartitionSpec as P

HL = 512
HR = 64
HK = 576
KP = 640
HEADS = 8
TOK = 128
HALF = 320
MESH = pl.DeviceIdType.MESH
BF = jnp.bfloat16
F32 = jnp.float32

score_scale = 192.0 ** (-0.5)

PLANE = sorted(((dx, dy) for dx in range(4) for dy in range(4) if (dx, dy) != (0, 0)), key=lambda o: (-min(o[0], 4 - o[0]) - min(o[1], 4 - o[1]), o))
NEAR_Z = sorted((d for d in range(1, 16) if d < 7 or d > 9), key=lambda k: (-min(k, 16 - k), k))


def rows16(start, size):
    return pl.ds(pl.multiple_of(start, 16), size)


def remote(src, dst, send, recv, where):
    return pltpu.make_async_remote_copy(
        src_ref=src, dst_ref=dst, send_sem=send, recv_sem=recv, device_id=where, device_id_type=MESH
    )


def pack(block):
    pad = jnp.zeros((8, 128), F32)
    tail = jnp.concatenate([block[:, 384:640], pad], axis=1)
    return jnp.concatenate([block[:, 0:384], tail], axis=0)


def unpack(block):
    return jnp.concatenate([block[0:8, :], block[8:16, 0:256]], axis=1)


def kernel(
    q_hbm, tr_hbm, own_hbm, g_hbm, vis_hbm,
    gq_hbm, gt_hbm, go_hbm,
    tr_ref, own_ref, vis_ref, gt_ref, got_ref,
    q_s, qo_s, g_s, k_s, bias_s, s_s, dp_s, p_s, d_s, o_s,
    zg_src, zg_buf, kx_src, kx_buf, kacc, xr_src, xr_buf, zr_src, zr_buf, fin_src, fin_buf,
    os_src, oz_buf, ow_buf,
    lq, lo, lg, lw, ls, lf,
    zg_send, zg_recv, xg_send, xg_recv, cg_send, cg_recv, kx_send, kx_recv,
    xr_send, xr_recv, zr_send, zr_recv, fin_send, fin_recv, oz_send, oz_recv, og_send, og_recv, fo_send, fo_recv, relay,
):
    g = lax.axis_index("grp")
    t = lax.axis_index("tp")
    xy, zh = g // 4, g % 4
    zl, core = t // 2, t % 2
    z = zh * 4 + zl
    other = 1 - core
    sib = (g, zl * 2 + other)

    def plane(n, sign):
        dx, dy = PLANE[n]
        return ((xy // 4 + 4 + sign * dx) % 4) * 4 + (xy % 4 + 4 + sign * dy) % 4

    def at_xy(n):
        return (plane(n, 1) * 4 + zh, t)

    def at_z(zz):
        return (xy * 4 + zz // 4, (zz % 4) * 2 + core)

    small = [
        pltpu.make_async_copy(src, dst, ls.at[i])
        for i, (src, dst) in enumerate([(tr_hbm, tr_ref), (own_hbm, own_ref), (vis_hbm, vis_ref)])
    ]
    for copy in small:
        copy.start()

    barrier = pltpu.get_barrier_semaphore()
    for k in NEAR_Z:
        pl.semaphore_signal(barrier, inc=1, device_id=at_z((z + k) % 16), device_id_type=MESH)
    for n in range(15):
        pl.semaphore_signal(barrier, inc=1, device_id=at_xy(n), device_id_type=MESH)
    pl.semaphore_signal(barrier, inc=1, device_id=sib, device_id_type=MESH)

    def load_q(hp):
        return pltpu.make_async_copy(
            q_hbm.at[:, pl.ds(hp * 2 * HK, KP)], q_s.at[pl.ds(hp * 256, TOK)], lq.at[hp]
        )

    def load_o(hp):
        return pltpu.make_async_copy(
            q_hbm.at[:, pl.ds(hp * 2 * HK + HL, KP)], qo_s.at[pl.ds(hp * TOK, TOK)], lo.at[hp]
        )

    def load_g(h):
        return pltpu.make_async_copy(
            g_hbm.at[:, pl.ds(h * HL, HL)], g_s.at[pl.ds(h * TOK, TOK)], lg.at[h]
        )

    small[0].wait()
    slab = jnp.concatenate([tr_ref[...].astype(F32), jnp.zeros((8, KP - HK), F32)], axis=1)
    zg_src[...] = pack(slab).astype(BF)
    mine = (zh // 2) == core

    pl.semaphore_wait(barrier, 28)

    def zg(d, up):
        zz = (z + d) % 16 if up else (z + 16 - d) % 16
        return remote(zg_src, zg_buf.at[zh], zg_send.at[d], zg_recv.at[zh], at_z(zz))

    def zg_from(src):
        return remote(zg_src, zg_buf.at[src], zg_send.at[0], zg_recv.at[src], (g, t))

    for chip, up in ((3, True), (0, False)):

        @pl.when(jnp.logical_and(mine, zl == chip))
        def _():
            for d in reversed(range(1, 7)):
                zg(d, up).start()

    @pl.when(mine)
    def _():
        zg_buf[zh] = zg_src[...]

    def zg_sent():
        for chip, up in ((3, True), (0, False)):

            @pl.when(jnp.logical_and(mine, zl == chip))
            def _():
                for d in range(1, 7):
                    zg(d, up).wait_send()

    drains = [zg_sent]

    pl.semaphore_signal(relay, inc=1, device_id=at_z((z + 10) % 16), device_id_type=MESH)

    for hp in range(HEADS // 2):
        load_q(hp).start()
        load_o(hp).start()
    for h in range(HEADS):
        load_g(h).start()
    small[1].wait()
    owns = own_ref[...].astype(F32).T.astype(BF)
    for cc in range(2):
        k_s[cc * HALF + 256 : (cc + 1) * HALF, :] = jnp.concatenate(
            [owns[cc * 64 : cc * 64 + 64, :], jnp.zeros((64, KP - HK), BF)], axis=1
        )
    small[2].wait()
    seen = vis_ref[...].reshape(1, TOK)
    low = jnp.float32(-1e30)
    for cc in range(2):
        row = lax.broadcasted_iota(jnp.int32, (256, TOK), 0)
        spot = (row // 16) * 32 + cc * 16 + row % 16
        bias_s[cc * HALF : cc * HALF + 256, :] = jnp.where(spot < seen, jnp.float32(0.0), low)
        row = lax.broadcasted_iota(jnp.int32, (64, TOK), 0) + cc * 64
        lane = lax.broadcasted_iota(jnp.int32, (64, TOK), 1)
        bias_s[cc * HALF + 256 : (cc + 1) * HALF, :] = jnp.where(row == lane, jnp.float32(0.0), low)

    for hp in range(HEADS // 2):
        load_q(hp).wait()
        load_o(hp).wait()
        odd = qo_s[hp * TOK : (hp + 1) * TOK, :].astype(F32)
        odd = jnp.concatenate([odd[:, 64:], odd[:, :64]], axis=1)
        q_s[hp * 256 + TOK : hp * 256 + 256, :] = odd.astype(BF)
    for h in range(HEADS):
        load_g(h).wait()

    for i in range(2):
        src = core * 2 + i

        @pl.when(src != zh)
        def _():
            zg_from(src).wait_recv()

    pair = jnp.concatenate([unpack(zg_buf[core * 2 + i].astype(F32)) for i in range(2)], axis=0)
    k_s[rows16(core * HALF + xy * 16, 16), :] = pair.astype(BF)

    def xg(k):
        block = k_s.at[rows16(core * HALF + xy * 16, 16)]
        return remote(block, block, xg_send.at[k], xg_recv.at[k], at_xy(k))

    def cg(n):
        spot = xy if n == 15 else plane(n, -1)
        block = k_s.at[rows16(core * HALF + spot * 16, 16)]
        return remote(block, block, cg_send.at[n], cg_recv.at[n], sib)

    def xg_got(n):
        block = k_s.at[rows16(core * HALF + plane(n, -1) * 16, 16)]
        return remote(block, block, xg_send.at[n], xg_recv.at[n], at_xy(n))

    def cg_got(n):
        spot = xy if n == 15 else plane(n, -1)
        block = k_s.at[rows16(other * HALF + spot * 16, 16)]
        return remote(block, block, cg_send.at[n], cg_recv.at[n], sib)

    for n in range(15):
        xg(n).start()
    cg(15).start()
    for n in reversed(range(15)):
        xg_got(n).wait_recv()
        cg(n).start()
    def keys_sent():
        cg(15).wait_send()
        for n in range(15):
            xg(n).wait_send()
            cg(n).wait_send()

    drains.append(keys_sent)

    nt = (((1,), (1,)), ((), ()))
    own_rows, other_rows = rows16(core * HALF, HALF), rows16(other * HALF, HALF)

    def scores(rows, at):
        s = lax.dot_general(k_s[rows, :], q_s[at, :], nt, preferred_element_type=F32)
        dp = lax.dot_general(k_s[rows, 0:HL], g_s[at, :], nt, preferred_element_type=F32)
        bias = jnp.concatenate([bias_s[rows, :], bias_s[rows, :]], axis=1)
        return s * score_scale + bias, dp

    for hp in range(HEADS // 2):
        at = slice(hp * 256, hp * 256 + 256)
        s_s[:, at], dp_s[:, at] = scores(own_rows, at)

    for n in reversed(range(16)):
        cg_got(n).wait_recv()

    for hp in range(HEADS // 2):
        at = slice(hp * 256, hp * 256 + 256)
        s1, dp1 = scores(other_rows, at)
        s0, dp0 = s_s[:, at], dp_s[:, at]
        top = jnp.maximum(jnp.max(s0, axis=0, keepdims=True), jnp.max(s1, axis=0, keepdims=True))
        e0, e1 = jnp.exp(s0 - top), jnp.exp(s1 - top)
        inv = 1.0 / (jnp.sum(e0, axis=0, keepdims=True) + jnp.sum(e1, axis=0, keepdims=True))
        p0, p1 = e0 * inv, e1 * inv
        delta = jnp.sum(p0 * dp0, axis=0, keepdims=True) + jnp.sum(p1 * dp1, axis=0, keepdims=True)
        p_s[own_rows, at] = p0.astype(BF)
        p_s[other_rows, at] = p1.astype(BF)
        d_s[own_rows, at] = (p0 * (dp0 - delta)).astype(BF)
        d_s[other_rows, at] = (p1 * (dp1 - delta)).astype(BF)

    def key_grad(half):
        at = rows16(half * HALF, HALF)
        a = jnp.dot(d_s[at, :], q_s[...], preferred_element_type=F32) * score_scale
        b = jnp.dot(p_s[at, :], g_s[...], preferred_element_type=F32)
        return jnp.concatenate([a[:, 0:HL] + b, a[:, HL:]], axis=1)

    kx_src[...] = key_grad(other).astype(BF)
    kx = remote(kx_src, kx_buf, kx_send, kx_recv, sib)
    kx.start()
    drains.append(kx.wait_send)
    kacc[...] = key_grad(core)
    kx.wait_recv()
    total = kacc[...] + kx_buf[...].astype(F32)
    kacc[...] = total
    xr_src[...] = total[0:256, :].astype(BF)
    os_src[...] = total[256:HALF, :].astype(BF)

    def xr(n):
        block = xr_src.at[rows16(plane(n, 1) * 16, 16)]
        return remote(block, xr_buf.at[n], xr_send.at[n], xr_recv.at[n], at_xy(n))

    for n in range(15):
        xr(n).start()

    def oz(k):
        to = (zl + k) % 4
        return remote(os_src.at[rows16(to * 16, 16)], oz_buf.at[zl], oz_send.at[k], oz_recv.at[zl], (g, to * 2 + core))

    def oz_from(k):
        src = (zl + k) % 4
        return remote(os_src.at[0:16], oz_buf.at[src], oz_send.at[k], oz_recv.at[src], (g, src * 2 + core))

    def og(k):
        block = ow_buf.at[rows16(core * 64 + zl * 16, 16)]
        return remote(block, block, og_send.at[k], og_recv.at[zl], (g, ((zl + k) % 4) * 2 + core))

    def og_from(k):
        src = (zl + k) % 4
        block = ow_buf.at[rows16(core * 64 + src * 16, 16)]
        return remote(block, block, og_send.at[k], og_recv.at[src], (g, src * 2 + core))

    for k in range(1, 4):
        oz(k).start()
    oz_buf[zl] = os_src[rows16(zl * 16, 16), :]

    def sums_sent():
        for n in range(15):
            xr(n).wait_send()
        for k in range(1, 4):
            oz(k).wait_send()

    drains.append(sums_sent)

    def store_q(hp):
        return pltpu.make_async_copy(
            o_s.at[:, pl.ds(pl.multiple_of(hp * 2 * HK, 128), 2 * HK)],
            gq_hbm.at[:, pl.ds(pl.multiple_of(hp * 2 * HK, 128), 2 * HK)],
            lw.at[hp],
        )

    @pl.loop(0, HEADS // 2)
    def _(hp):
        at = pl.ds(pl.multiple_of(hp * 256, 256), 256)
        tn = (((0,), (0,)), ((), ()))
        gq = lax.dot_general(d_s[:, at], k_s[...], tn, preferred_element_type=F32) * score_scale
        even, odd = gq[0:TOK, :], gq[TOK:, :]
        odd = jnp.concatenate([odd[:, HK:], odd[:, :HK]], axis=1)
        joint = jnp.concatenate([even[:, 0:HL], even[:, HL:] + odd[:, 0:128], odd[:, 128:]], axis=1)
        o_s[:, pl.ds(pl.multiple_of(hp * 2 * HK, 128), 2 * HK)] = joint.astype(BF)
        store_q(hp).start()

    drains.append(lambda: [store_q(hp).wait() for hp in range(HEADS // 2)])
    for k in range(1, 4):
        oz_from(k).wait_recv()
    own_sum = oz_buf[0].astype(F32)
    for a in range(1, 4):
        own_sum = own_sum + oz_buf[a].astype(F32)
    ow_buf[rows16(core * 64 + zl * 16, 16), :] = own_sum.astype(BF)
    for k in range(1, 4):
        og(k).start()
    drains.append(lambda: [og(k).wait_send() for k in range(1, 4)])

    total = kacc[rows16(xy * 16, 16), :]
    for n in reversed(range(15)):
        xr(n).wait_recv()
        total = total + xr_buf[n].astype(F32)
    zr_src[0] = pack(total[0:8, :]).astype(BF)
    zr_src[1] = pack(total[8:16, :]).astype(BF)

    pl.semaphore_wait(relay, 1)

    def zr(i, a):
        to = (core * 2 + i) * 4 + a
        return remote(zr_src.at[i], zr_buf.at[z], zr_send.at[i * 4 + a], zr_recv.at[z], at_z(to))

    def zr_from(src):
        return remote(zr_src.at[0], zr_buf.at[src], zr_send.at[0], zr_recv.at[src], at_z(src))

    for i in range(2):
        for a in range(4):

            @pl.when((core * 2 + i) * 4 + a != z)
            def _():
                zr(i, a).start()

    def slabs_sent():
        for i in range(2):
            for a in range(4):

                @pl.when((core * 2 + i) * 4 + a != z)
                def _():
                    zr(i, a).wait_send()

    drains.append(slabs_sent)

    for k in range(1, 4):
        og_from(k).wait_recv()
    own_half = ow_buf.at[rows16(core * 64, 64)]
    fo = remote(own_half, own_half, fo_send, fo_recv, sib)
    fo.start()
    drains.append(fo.wait_send)
    own_half = ow_buf.at[rows16(other * 64, 64)]
    remote(own_half, own_half, fo_send, fo_recv, sib).wait_recv()
    got_ref[...] = ow_buf[...].astype(F32).T[0:HK, :]
    store_go = pltpu.make_async_copy(got_ref, go_hbm, lf.at[0])
    store_go.start()
    drains.append(store_go.wait)

    fin = remote(fin_src, fin_buf, fin_send, fin_recv, sib)

    @pl.when(mine)
    def _():
        zr_buf[z] = zr_src[zh % 2]
        total = jnp.zeros((16, 384), F32)
        for src in range(16):

            @pl.when(z != src)
            def _():
                zr_from(src).wait_recv()

            total = total + zr_buf[src].astype(F32)
        whole = unpack(total)
        fin_src[...] = whole
        fin.start()
        gt_ref[...] = whole[:, 0:HK]
        fin.wait_send()

    @pl.when(jnp.logical_not(mine))
    def _():
        fin.wait_recv()
        gt_ref[...] = fin_buf[:, 0:HK]

    store_gt = pltpu.make_async_copy(gt_ref, gt_hbm, lf.at[1])
    store_gt.start()
    drains.append(store_gt.wait)

    for drain in drains:
        drain()


def finish(q_in, t_in, o_in, q_out, t_out, o_out, q_s, t_s, o_s, sem, sem_out):
    pieces = [(q_in.at[pl.ds(i * 32, 32)], q_s.at[pl.ds(i * 32, 32)], q_out.at[pl.ds(i * 32, 32)]) for i in range(4)]
    pieces += [(o_in, o_s, o_out), (t_in, t_s, t_out)]
    loads = [pltpu.make_async_copy(p[0], p[1], sem.at[i]) for i, p in enumerate(pieces)]
    stores = [pltpu.make_async_copy(p[1], p[2], sem_out.at[i]) for i, p in enumerate(pieces)]
    for c in loads:
        c.start()
    for load, store in zip(loads, stores):
        load.wait()
        store.start()
    for c in stores:
        c.wait()


def per_device(queries, trunk, own, grad_out, visible):
    hbm = pl.BlockSpec(memory_space=pl.ANY)
    dma = pltpu.SemaphoreType.DMA
    grad_query, grad_trunk, grad_own = pl.pallas_call(
        kernel,
        out_shape=(
            jax.ShapeDtypeStruct((TOK, HEADS * HK), BF),
            jax.ShapeDtypeStruct((8, HK), F32),
            jax.ShapeDtypeStruct((HK, TOK), F32),
        ),
        in_specs=[hbm] * 5,
        out_specs=(hbm,) * 3,
        scratch_shapes=[
            pltpu.VMEM((8, HK), BF),
            pltpu.VMEM((HK, TOK), BF),
            pltpu.VMEM((TOK,), jnp.int32),
            pltpu.VMEM((8, HK), F32),
            pltpu.VMEM((HK, TOK), F32),
            pltpu.VMEM((HEADS * TOK, KP), BF),
            pltpu.VMEM((HEADS // 2 * TOK, KP), BF),
            pltpu.VMEM((HEADS * TOK, HL), BF),
            pltpu.VMEM((2 * HALF, KP), BF),
            pltpu.VMEM((2 * HALF, TOK), F32),
            pltpu.VMEM((HALF, HEADS * TOK), F32),
            pltpu.VMEM((HALF, HEADS * TOK), F32),
            pltpu.VMEM((2 * HALF, HEADS * TOK), BF),
            pltpu.VMEM((2 * HALF, HEADS * TOK), BF),
            pltpu.VMEM((TOK, HEADS * HK), BF),
            pltpu.VMEM((16, 384), BF),
            pltpu.VMEM((4, 16, 384), BF),
            pltpu.VMEM((HALF, KP), BF),
            pltpu.VMEM((HALF, KP), BF),
            pltpu.VMEM((HALF, KP), F32),
            pltpu.VMEM((256, KP), BF),
            pltpu.VMEM((16, 16, KP), BF),
            pltpu.VMEM((2, 16, 384), BF),
            pltpu.VMEM((16, 16, 384), BF),
            pltpu.VMEM((8, KP), F32),
            pltpu.VMEM((8, KP), F32),
            pltpu.VMEM((64, KP), BF),
            pltpu.VMEM((4, 16, KP), BF),
            pltpu.VMEM((TOK, KP), BF),
            dma((4,)), dma((4,)), dma((8,)), dma((4,)), dma((3,)), dma((2,)),
            dma((8,)), dma((4,)),
            dma((16,)), dma((16,)),
            dma((16,)), dma((16,)),
            dma, dma,
            dma((16,)), dma((16,)),
            dma((8,)), dma((16,)),
            dma, dma,
            dma((4,)), dma((4,)), dma((4,)), dma((4,)),
            dma, dma,
            pltpu.SemaphoreType.REGULAR,
        ],
        compiler_params=pltpu.CompilerParams(
            collective_id=0, has_side_effects=True, vmem_limit_bytes=60 * 1024 * 1024
        ),
        cost_estimate=pl.CostEstimate(flops=3860000000, bytes_accessed=4500000, transcendentals=655360),
    )(queries, trunk, own.T, grad_out, visible)
    outs = [jax.ShapeDtypeStruct(a.shape, a.dtype) for a in (grad_query, grad_trunk, grad_own)]
    grad_query, grad_trunk, grad_own = pl.pallas_call(
        finish,
        out_shape=outs,
        in_specs=[hbm] * 3,
        out_specs=[hbm] * 3,
        scratch_shapes=[pltpu.VMEM(a.shape, a.dtype) for a in outs] + [dma((6,)), dma((6,))],
        compiler_params=pltpu.CompilerParams(vmem_limit_bytes=60 * 1024 * 1024),
    )(grad_query, grad_trunk, grad_own)
    return grad_query, grad_trunk, grad_own.T


def solution(mesh):
    in_specs = (P("grp", "tp"), P("grp", None), P("grp", None), P("grp", "tp"), P("grp"))
    out_specs = (P("grp", "tp"), P("grp", None), P("grp", None))
    return jax.shard_map(
        per_device, mesh=mesh, in_specs=in_specs, out_specs=out_specs, check_vma=False
    )
```

```python
import jax
import jax.numpy as jnp
from jax import lax
from jax.experimental import pallas as pl
from jax.experimental.pallas import tpu as pltpu
from jax.sharding import PartitionSpec as P

HL = 512
HR = 64
HK = 576
KP = 640
HEADS = 8
TOK = 128
HALF = 256
ROWS = 640
MESH = pl.DeviceIdType.MESH
BF = jnp.bfloat16
F32 = jnp.float32

score_scale = 192.0 ** (-0.5)
log2e = 1.4426950408889634

PLANE = sorted(((dx, dy) for dx in range(4) for dy in range(4) if (dx, dy) != (0, 0)), key=lambda o: (-min(o[0], 4 - o[0]) - min(o[1], 4 - o[1]), o))
NEAR_Z = sorted((d for d in range(1, 16) if d < 7 or d > 9), key=lambda k: (-min(k, 16 - k), k))


def rows16(start, size):
    return pl.ds(pl.multiple_of(start, 16), size)


def remote(src, dst, send, recv, where):
    return pltpu.make_async_remote_copy(
        src_ref=src, dst_ref=dst, send_sem=send, recv_sem=recv, device_id=where, device_id_type=MESH
    )


def pack(block):
    pad = jnp.zeros((8, 128), F32)
    tail = jnp.concatenate([block[:, 384:640], pad], axis=1)
    return jnp.concatenate([block[:, 0:384], tail], axis=0)


def unpack(block):
    return jnp.concatenate([block[0:8, :], block[8:16, 0:256]], axis=1)


def kernel(
    q_hbm, tr_hbm, own_hbm, g_hbm, vis_hbm,
    gq_hbm, gt_hbm, go_hbm,
    tr_ref, own_ref, vis_ref, gt_ref, got_ref,
    q_s, qo_s, g_s, k_s, bias_s, s_s, dp_s, p_s, d_s, o_s,
    zg_src, zg_buf, kx_src, kx_buf, kacc, ko_src, ko_buf, ko_acc, xr_src, xr_buf, zr_src, zr_buf, fin_src, fin_buf,
    os_src, oz_buf, ow_buf,
    lq, lo, lg, lw, ls, lf,
    zg_send, zg_recv, xg_send, xg_recv, cg_send, cg_recv, kx_send, kx_recv, ko_send, ko_recv,
    xr_send, xr_recv, zr_send, zr_recv, fin_send, fin_recv, oz_send, oz_recv, og_send, og_recv, fo_send, fo_recv, relay,
):
    g = lax.axis_index("grp")
    t = lax.axis_index("tp")
    xy, zh = g // 4, g % 4
    zl, core = t // 2, t % 2
    z = zh * 4 + zl
    other = 1 - core
    sib = (g, zl * 2 + other)

    def plane(n, sign):
        dx, dy = PLANE[n]
        return ((xy // 4 + 4 + sign * dx) % 4) * 4 + (xy % 4 + 4 + sign * dy) % 4

    def at_xy(n):
        return (plane(n, 1) * 4 + zh, t)

    def at_z(zz):
        return (xy * 4 + zz // 4, (zz % 4) * 2 + core)

    small = [
        pltpu.make_async_copy(src, dst, ls.at[i])
        for i, (src, dst) in enumerate([(tr_hbm, tr_ref), (own_hbm, own_ref), (vis_hbm, vis_ref)])
    ]
    for copy in small:
        copy.start()

    barrier = pltpu.get_barrier_semaphore()
    for k in NEAR_Z:
        pl.semaphore_signal(barrier, inc=1, device_id=at_z((z + k) % 16), device_id_type=MESH)
    for n in range(15):
        pl.semaphore_signal(barrier, inc=1, device_id=at_xy(n), device_id_type=MESH)
    pl.semaphore_signal(barrier, inc=1, device_id=sib, device_id_type=MESH)

    def load_q(hp):
        return pltpu.make_async_copy(
            q_hbm.at[:, pl.ds(hp * 2 * HK, KP)], q_s.at[pl.ds(hp * 256, TOK)], lq.at[hp]
        )

    def load_o(hp):
        return pltpu.make_async_copy(
            q_hbm.at[:, pl.ds(hp * 2 * HK + HL, KP)], qo_s.at[pl.ds(hp * TOK, TOK)], lo.at[hp]
        )

    def load_g(h):
        return pltpu.make_async_copy(
            g_hbm.at[:, pl.ds(h * HL, HL)], g_s.at[pl.ds(h * TOK, TOK)], lg.at[h]
        )

    small[0].wait()
    slab = jnp.concatenate([tr_ref[...].astype(F32), jnp.zeros((8, KP - HK), F32)], axis=1)
    zg_src[...] = pack(slab).astype(BF)
    mine = (zh // 2) == core

    pl.semaphore_wait(barrier, 28)

    def zg(d, up):
        zz = (z + d) % 16 if up else (z + 16 - d) % 16
        return remote(zg_src, zg_buf.at[zh], zg_send.at[d], zg_recv.at[zh], at_z(zz))

    def zg_from(src):
        return remote(zg_src, zg_buf.at[src], zg_send.at[0], zg_recv.at[src], (g, t))

    for chip, up in ((3, True), (0, False)):

        @pl.when(jnp.logical_and(mine, zl == chip))
        def _():
            for d in reversed(range(1, 7)):
                zg(d, up).start()

    @pl.when(mine)
    def _():
        zg_buf[zh] = zg_src[...]

    def zg_sent():
        for chip, up in ((3, True), (0, False)):

            @pl.when(jnp.logical_and(mine, zl == chip))
            def _():
                for d in range(1, 7):
                    zg(d, up).wait_send()

    drains = [zg_sent]

    pl.semaphore_signal(relay, inc=1, device_id=at_z((z + 10) % 16), device_id_type=MESH)

    for hp in range(HEADS // 2):
        load_q(hp).start()
        load_o(hp).start()
    for h in range(HEADS):
        load_g(h).start()
    small[1].wait()
    owns = own_ref[...].astype(F32).T.astype(BF)
    k_s[2 * HALF : ROWS, :] = jnp.concatenate([owns, jnp.zeros((TOK, KP - HK), BF)], axis=1)
    small[2].wait()
    seen = vis_ref[...].reshape(1, TOK)
    low = jnp.float32(-1e30)
    for cc in range(2):
        row = lax.broadcasted_iota(jnp.int32, (HALF, TOK), 0)
        spot = (row // 16) * 32 + cc * 16 + row % 16
        bias_s[cc * HALF : (cc + 1) * HALF, :] = jnp.where(spot < seen, jnp.float32(0.0), low)
    row = lax.broadcasted_iota(jnp.int32, (TOK, TOK), 0)
    lane = lax.broadcasted_iota(jnp.int32, (TOK, TOK), 1)
    bias_s[2 * HALF : ROWS, :] = jnp.where(row == lane, jnp.float32(0.0), low)

    for hp in range(HEADS // 2):
        load_q(hp).wait()
        load_o(hp).wait()
        odd = qo_s[hp * TOK : (hp + 1) * TOK, :].astype(F32)
        odd = jnp.concatenate([odd[:, 64:], odd[:, :64]], axis=1)
        q_s[hp * 256 + TOK : hp * 256 + 256, :] = odd.astype(BF)
    for h in range(HEADS):
        load_g(h).wait()

    nt = (((1,), (1,)), ((), ()))

    def scores(rows):
        for hp in range(HEADS // 2):
            at = slice(hp * 256, hp * 256 + 256)
            s = lax.dot_general(k_s[rows, :], q_s[at, :], nt, preferred_element_type=F32)
            bias = jnp.concatenate([bias_s[rows, :], bias_s[rows, :]], axis=1)
            s_s[rows, at] = s * (score_scale * log2e) + bias
            dp_s[rows, at] = lax.dot_general(k_s[rows, 0:HL], g_s[at, :], nt, preferred_element_type=F32)

    scores(slice(2 * HALF, ROWS))

    for i in range(2):
        src = core * 2 + i

        @pl.when(src != zh)
        def _():
            zg_from(src).wait_recv()

    pair = jnp.concatenate([unpack(zg_buf[core * 2 + i].astype(F32)) for i in range(2)], axis=0)
    k_s[rows16(core * HALF + xy * 16, 16), :] = pair.astype(BF)

    def xg(k):
        block = k_s.at[rows16(core * HALF + xy * 16, 16)]
        return remote(block, block, xg_send, xg_recv.at[k], at_xy(k))

    def cg(n):
        spot = xy if n == 15 else plane(n, -1)
        block = k_s.at[rows16(core * HALF + spot * 16, 16)]
        return remote(block, block, cg_send, cg_recv, sib)

    def xg_got(n):
        block = k_s.at[rows16(core * HALF + plane(n, -1) * 16, 16)]
        return remote(block, block, xg_send, xg_recv.at[n], at_xy(n))

    for n in range(15):
        xg(n).start()
    cg(15).start()
    for n in reversed(range(15)):
        xg_got(n).wait_recv()
        cg(n).start()
    own_rows, other_rows = rows16(core * HALF, HALF), rows16(other * HALF, HALF)

    def keys_sent():
        most = k_s.at[0:240]
        remote(most, most, xg_send, xg_recv.at[0], sib).wait_send()
        half = k_s.at[own_rows]
        remote(half, half, cg_send, cg_recv, sib).wait_send()

    drains.append(keys_sent)

    scores(own_rows)
    half = k_s.at[other_rows]
    remote(half, half, cg_send, cg_recv, sib).wait_recv()
    scores(other_rows)

    for hp in range(HEADS // 2):
        at = slice(hp * 256, hp * 256 + 256)
        s, dp = s_s[:, at], dp_s[:, at]
        e = jnp.exp2(s - jnp.max(s, axis=0, keepdims=True))
        p = e * (1.0 / jnp.sum(e, axis=0, keepdims=True))
        delta = jnp.sum(p * dp, axis=0, keepdims=True)
        p_s[:, at] = p.astype(BF)
        d_s[:, at] = (p * (dp - delta)).astype(BF)

    def key_grad(rows):
        a = jnp.dot(d_s[rows, :], q_s[...], preferred_element_type=F32) * score_scale
        b = jnp.dot(p_s[rows, :], g_s[...], preferred_element_type=F32)
        return jnp.concatenate([a[:, 0:HL] + b, a[:, HL:]], axis=1)

    kx_src[...] = key_grad(other_rows).astype(BF)
    kx = remote(kx_src, kx_buf, kx_send, kx_recv, sib)
    kx.start()
    drains.append(kx.wait_send)
    kacc[...] = key_grad(own_rows)
    ko_acc[...] = key_grad(slice(2 * HALF, ROWS))
    ko_src[...] = ko_acc[rows16(other * 64, 64), :].astype(BF)
    ko = remote(ko_src, ko_buf, ko_send, ko_recv, sib)
    ko.start()
    drains.append(ko.wait_send)
    kx.wait_recv()
    total = kacc[...] + kx_buf[...].astype(F32)
    kacc[...] = total
    xr_src[...] = total.astype(BF)

    def xr(n):
        block = xr_src.at[rows16(plane(n, 1) * 16, 16)]
        return remote(block, xr_buf.at[n], xr_send, xr_recv, at_xy(n))

    for n in range(15):
        xr(n).start()

    def oz(k):
        to = (zl + k) % 4
        return remote(os_src.at[rows16(to * 16, 16)], oz_buf.at[zl], oz_send.at[k], oz_recv.at[zl], (g, to * 2 + core))

    def oz_from(k):
        src = (zl + k) % 4
        return remote(os_src.at[0:16], oz_buf.at[src], oz_send.at[k], oz_recv.at[src], (g, src * 2 + core))

    def og(k):
        block = ow_buf.at[rows16(core * 64 + zl * 16, 16)]
        return remote(block, block, og_send.at[k], og_recv.at[zl], (g, ((zl + k) % 4) * 2 + core))

    def og_from(k):
        src = (zl + k) % 4
        block = ow_buf.at[rows16(core * 64 + src * 16, 16)]
        return remote(block, block, og_send.at[k], og_recv.at[src], (g, src * 2 + core))

    def sums_sent():
        most = xr_src.at[0:240]
        remote(most, most, xr_send, xr_recv, sib).wait_send()
        for k in range(1, 4):
            oz(k).wait_send()

    drains.append(sums_sent)

    def store_q(hp):
        return pltpu.make_async_copy(
            o_s.at[:, pl.ds(pl.multiple_of(hp * 2 * HK, 128), 2 * HK)],
            gq_hbm.at[:, pl.ds(pl.multiple_of(hp * 2 * HK, 128), 2 * HK)],
            lw.at[hp],
        )

    def query_grad(hp):
        at = pl.ds(pl.multiple_of(hp * 256, 256), 256)
        tn = (((0,), (0,)), ((), ()))
        gq = lax.dot_general(d_s[:, at], k_s[...], tn, preferred_element_type=F32) * score_scale
        even, odd = gq[0:TOK, :], gq[TOK:, :]
        odd = jnp.concatenate([odd[:, HK:], odd[:, :HK]], axis=1)
        joint = jnp.concatenate([even[:, 0:HL], even[:, HL:] + odd[:, 0:128], odd[:, 128:]], axis=1)
        o_s[:, pl.ds(pl.multiple_of(hp * 2 * HK, 128), 2 * HK)] = joint.astype(BF)
        store_q(hp).start()

    query_grad(0)
    ko.wait_recv()
    os_src[...] = (ko_acc[rows16(core * 64, 64), :] + ko_buf[...].astype(F32)).astype(BF)
    for k in range(1, 4):
        oz(k).start()
    oz_buf[zl] = os_src[rows16(zl * 16, 16), :]
    pl.loop(1, HEADS // 2)(query_grad)

    drains.append(lambda: [store_q(hp).wait() for hp in range(HEADS // 2)])
    total = kacc[rows16(xy * 16, 16), :]
    remote(xr_buf, xr_buf, xr_send, xr_recv, sib).wait_recv()
    for n in range(15):
        total = total + xr_buf[n].astype(F32)
    zr_src[0] = pack(total[0:8, :]).astype(BF)
    zr_src[1] = pack(total[8:16, :]).astype(BF)

    pl.semaphore_wait(relay, 1)

    def zr(i, a):
        to = (core * 2 + i) * 4 + a
        return remote(zr_src.at[i], zr_buf.at[z], zr_send, zr_recv, at_z(to))

    for i in range(2):
        for a in range(4):

            @pl.when((core * 2 + i) * 4 + a != z)
            def _():
                zr(i, a).start()

    def slabs_sent():
        @pl.when(mine)
        def _():
            remote(zr_buf.at[0:7], zr_buf.at[0:7], zr_send, zr_recv, sib).wait_send()

        @pl.when(jnp.logical_not(mine))
        def _():
            remote(zr_buf.at[0:8], zr_buf.at[0:8], zr_send, zr_recv, sib).wait_send()


    for k in range(1, 4):
        oz_from(k).wait_recv()
    own_sum = oz_buf[0].astype(F32)
    for a in range(1, 4):
        own_sum = own_sum + oz_buf[a].astype(F32)
    ow_buf[rows16(core * 64 + zl * 16, 16), :] = own_sum.astype(BF)
    for k in range(1, 4):
        og(k).start()
    drains.append(lambda: [og(k).wait_send() for k in range(1, 4)])

    for k in range(1, 4):
        og_from(k).wait_recv()
    own_half = ow_buf.at[rows16(core * 64, 64)]
    fo = remote(own_half, own_half, fo_send, fo_recv, sib)
    fo.start()
    drains.append(fo.wait_send)
    own_half = ow_buf.at[rows16(other * 64, 64)]
    remote(own_half, own_half, fo_send, fo_recv, sib).wait_recv()
    got_ref[...] = ow_buf[...].astype(F32).T[0:HK, :]
    store_go = pltpu.make_async_copy(got_ref, go_hbm, lf.at[0])
    store_go.start()
    drains.append(store_go.wait)

    for drain in drains:
        drain()

    fin = remote(fin_src, fin_buf, fin_send, fin_recv, sib)

    @pl.when(mine)
    def _():
        zr_buf[z] = zr_src[zh % 2]
        remote(zr_buf.at[0:15], zr_buf.at[0:15], zr_send, zr_recv, sib).wait_recv()
        total = jnp.zeros((16, 384), F32)
        for src in range(16):
            total = total + zr_buf[src].astype(F32)
        whole = unpack(total)
        fin_src[...] = whole
        fin.start()
        gt_ref[...] = whole[:, 0:HK]

    @pl.when(jnp.logical_not(mine))
    def _():
        fin.wait_recv()
        gt_ref[...] = fin_buf[:, 0:HK]

    store_gt = pltpu.make_async_copy(gt_ref, gt_hbm, lf.at[1])
    store_gt.start()
    slabs_sent()

    @pl.when(mine)
    def _():
        fin.wait_send()

    store_gt.wait()


def finish(q_in, t_in, o_in, q_out, t_out, o_out, q_s, t_s, o_s, sem, sem_out):
    pieces = [(q_in.at[pl.ds(i * 32, 32)], q_s.at[pl.ds(i * 32, 32)], q_out.at[pl.ds(i * 32, 32)]) for i in range(4)]
    pieces += [(o_in, o_s, o_out), (t_in, t_s, t_out)]
    loads = [pltpu.make_async_copy(p[0], p[1], sem.at[i]) for i, p in enumerate(pieces)]
    stores = [pltpu.make_async_copy(p[1], p[2], sem_out.at[i]) for i, p in enumerate(pieces)]
    for c in loads:
        c.start()
    for load, store in zip(loads, stores):
        load.wait()
        store.start()
    for c in stores:
        c.wait()


def per_device(queries, trunk, own, grad_out, visible):
    hbm = pl.BlockSpec(memory_space=pl.ANY)
    dma = pltpu.SemaphoreType.DMA
    grad_query, grad_trunk, grad_own = pl.pallas_call(
        kernel,
        out_shape=(
            jax.ShapeDtypeStruct((TOK, HEADS * HK), BF),
            jax.ShapeDtypeStruct((8, HK), F32),
            jax.ShapeDtypeStruct((HK, TOK), F32),
        ),
        in_specs=[hbm] * 5,
        out_specs=(hbm,) * 3,
        scratch_shapes=[
            pltpu.VMEM((8, HK), BF),
            pltpu.VMEM((HK, TOK), BF),
            pltpu.VMEM((TOK,), jnp.int32),
            pltpu.VMEM((8, HK), F32),
            pltpu.VMEM((HK, TOK), F32),
            pltpu.VMEM((HEADS * TOK, KP), BF),
            pltpu.VMEM((HEADS // 2 * TOK, KP), BF),
            pltpu.VMEM((HEADS * TOK, HL), BF),
            pltpu.VMEM((ROWS, KP), BF),
            pltpu.VMEM((ROWS, TOK), F32),
            pltpu.VMEM((ROWS, HEADS * TOK), F32),
            pltpu.VMEM((ROWS, HEADS * TOK), F32),
            pltpu.VMEM((ROWS, HEADS * TOK), BF),
            pltpu.VMEM((ROWS, HEADS * TOK), BF),
            pltpu.VMEM((TOK, HEADS * HK), BF),
            pltpu.VMEM((16, 384), BF),
            pltpu.VMEM((4, 16, 384), BF),
            pltpu.VMEM((HALF, KP), BF),
            pltpu.VMEM((HALF, KP), BF),
            pltpu.VMEM((HALF, KP), F32),
            pltpu.VMEM((64, KP), BF),
            pltpu.VMEM((64, KP), BF),
            pltpu.VMEM((TOK, KP), F32),
            pltpu.VMEM((HALF, KP), BF),
            pltpu.VMEM((15, 16, KP), BF),
            pltpu.VMEM((2, 16, 384), BF),
            pltpu.VMEM((16, 16, 384), BF),
            pltpu.VMEM((8, KP), F32),
            pltpu.VMEM((8, KP), F32),
            pltpu.VMEM((64, KP), BF),
            pltpu.VMEM((4, 16, KP), BF),
            pltpu.VMEM((TOK, KP), BF),
            dma((4,)), dma((4,)), dma((8,)), dma((4,)), dma((3,)), dma((2,)),
            dma((8,)), dma((4,)),
            dma, dma((16,)),
            dma, dma,
            dma, dma, dma, dma,
            dma, dma,
            dma, dma,
            dma, dma,
            dma((4,)), dma((4,)), dma((4,)), dma((4,)),
            dma, dma,
            pltpu.SemaphoreType.REGULAR,
        ],
        compiler_params=pltpu.CompilerParams(
            collective_id=0, has_side_effects=True, vmem_limit_bytes=60 * 1024 * 1024
        ),
        cost_estimate=pl.CostEstimate(flops=3860000000, bytes_accessed=4500000, transcendentals=655360),
    )(queries, trunk, own.T, grad_out, visible)
    outs = [jax.ShapeDtypeStruct(a.shape, a.dtype) for a in (grad_query, grad_trunk, grad_own)]
    grad_query, grad_trunk, grad_own = pl.pallas_call(
        finish,
        out_shape=outs,
        in_specs=[hbm] * 3,
        out_specs=[hbm] * 3,
        scratch_shapes=[pltpu.VMEM(a.shape, a.dtype) for a in outs] + [dma((6,)), dma((6,))],
        compiler_params=pltpu.CompilerParams(vmem_limit_bytes=60 * 1024 * 1024),
    )(grad_query, grad_trunk, grad_own)
    return grad_query, grad_trunk, grad_own.T


def solution(mesh):
    in_specs = (P("grp", "tp"), P("grp", None), P("grp", None), P("grp", "tp"), P("grp"))
    out_specs = (P("grp", "tp"), P("grp", None), P("grp", None))
    return jax.shard_map(
        per_device, mesh=mesh, in_specs=in_specs, out_specs=out_specs, check_vma=False
    )
```

```python
import functools

import jax
import jax.numpy as jnp
from jax import lax
from jax.experimental import pallas as pl
from jax.experimental.pallas import tpu as pltpu
from jax.sharding import PartitionSpec as P

HL = 512
HR = 64
HK = 576
KP = 640
HEADS = 8
TOK = 128
HALF = 256
ROWS = 640
MESH = pl.DeviceIdType.MESH
BF = jnp.bfloat16
F32 = jnp.float32

score_scale = 192.0 ** (-0.5)
log2e = 1.4426950408889634

PLANE = sorted(((dx, dy) for dx in range(4) for dy in range(4) if (dx, dy) != (0, 0)), key=lambda o: (-min(o[0], 4 - o[0]) - min(o[1], 4 - o[1]), o))
NEAR_Z = sorted((d for d in range(1, 16) if d < 7 or d > 9), key=lambda k: (-min(k, 16 - k), k))


def rows16(start, size):
    return pl.ds(pl.multiple_of(start, 16), size)


def remote(src, dst, send, recv, where):
    return pltpu.make_async_remote_copy(
        src_ref=src, dst_ref=dst, send_sem=send, recv_sem=recv, device_id=where, device_id_type=MESH
    )


def pack(block):
    pad = jnp.zeros((8, 128), F32)
    tail = jnp.concatenate([block[:, 384:640], pad], axis=1)
    return jnp.concatenate([block[:, 0:384], tail], axis=0)


def unpack(block):
    return jnp.concatenate([block[0:8, :], block[8:16, 0:256]], axis=1)


def kernel(
    q_hbm, tr_hbm, own_hbm, g_hbm, vis_hbm,
    gq_hbm, gt_hbm, go_hbm,
    tr_ref, own_ref, vis_ref, gt_ref, got_ref,
    q_s, qo_s, g_s, k_s, bias_s, s_s, dp_s, p_s, d_s, o_s,
    zg_src, zg_buf, kx_src, kx_buf, kacc, ko_src, ko_buf, ko_acc, xr_src, xr_buf, zr_src, zr_buf, fin_src, fin_buf,
    os_src, oz_buf, ow_buf,
    lq, lo, lg, lw, ls, lf,
    zg_send, zg_recv, xg_send, xg_recv, cg_send, cg_recv, kx_send, kx_recv, ko_send, ko_recv,
    xr_send, xr_recv, zr_send, zr_recv, fin_send, fin_recv, oz_send, oz_recv, og_send, og_recv, fo_send, fo_recv, relay,
):
    g = lax.axis_index("grp")
    t = lax.axis_index("tp")
    xy, zh = g // 4, g % 4
    zl, core = t // 2, t % 2
    z = zh * 4 + zl
    other = 1 - core
    sib = (g, zl * 2 + other)

    def plane(n, sign):
        dx, dy = PLANE[n]
        return ((xy // 4 + 4 + sign * dx) % 4) * 4 + (xy % 4 + 4 + sign * dy) % 4

    def at_xy(n):
        return (plane(n, 1) * 4 + zh, t)

    def at_z(zz):
        return (xy * 4 + zz // 4, (zz % 4) * 2 + core)

    small = [
        pltpu.make_async_copy(src, dst, ls.at[i])
        for i, (src, dst) in enumerate([(tr_hbm, tr_ref), (own_hbm, own_ref), (vis_hbm, vis_ref)])
    ]
    for copy in small:
        copy.start()

    barrier = pltpu.get_barrier_semaphore()
    for k in NEAR_Z:
        pl.semaphore_signal(barrier, inc=1, device_id=at_z((z + k) % 16), device_id_type=MESH)
    for n in range(15):
        pl.semaphore_signal(barrier, inc=1, device_id=at_xy(n), device_id_type=MESH)
    pl.semaphore_signal(barrier, inc=1, device_id=sib, device_id_type=MESH)

    def load_q(hp):
        return pltpu.make_async_copy(
            q_hbm.at[:, pl.ds(hp * 2 * HK, KP)], q_s.at[pl.ds(hp * 256, TOK)], lq.at[hp]
        )

    def load_o(hp):
        return pltpu.make_async_copy(
            q_hbm.at[:, pl.ds(hp * 2 * HK + HL, KP)], qo_s.at[pl.ds(hp * TOK, TOK)], lo.at[hp]
        )

    def load_g(h):
        return pltpu.make_async_copy(
            g_hbm.at[:, pl.ds(h * HL, HL)], g_s.at[pl.ds(h * TOK, TOK)], lg.at[h]
        )

    small[0].wait()
    slab = jnp.concatenate([tr_ref[...].astype(F32), jnp.zeros((8, KP - HK), F32)], axis=1)
    zg_src[...] = pack(slab).astype(BF)
    mine = (zh // 2) == core

    pl.semaphore_wait(barrier, 28)

    def zg(d, up):
        zz = (z + d) % 16 if up else (z + 16 - d) % 16
        return remote(zg_src, zg_buf.at[zh], zg_send.at[d], zg_recv.at[zh], at_z(zz))

    def zg_from(src):
        return remote(zg_src, zg_buf.at[src], zg_send.at[0], zg_recv.at[src], (g, t))

    for chip, up in ((3, True), (0, False)):

        @pl.when(jnp.logical_and(mine, zl == chip))
        def _():
            for d in reversed(range(1, 7)):
                zg(d, up).start()

    @pl.when(mine)
    def _():
        zg_buf[zh] = zg_src[...]

    def zg_sent():
        for chip, up in ((3, True), (0, False)):

            @pl.when(jnp.logical_and(mine, zl == chip))
            def _():
                for d in range(1, 7):
                    zg(d, up).wait_send()

    drains = [zg_sent]

    pl.semaphore_signal(relay, inc=1, device_id=at_z((z + 10) % 16), device_id_type=MESH)

    for hp in range(HEADS // 2):
        load_q(hp).start()
        load_o(hp).start()
    for h in range(HEADS):
        load_g(h).start()
    small[1].wait()
    owns = own_ref[...].astype(F32).T.astype(BF)
    k_s[2 * HALF : ROWS, :] = jnp.concatenate([owns, jnp.zeros((TOK, KP - HK), BF)], axis=1)
    small[2].wait()
    seen = vis_ref[...].reshape(1, TOK)
    low = jnp.float32(-1e30)
    for cc in range(2):
        row = lax.broadcasted_iota(jnp.int32, (HALF, TOK), 0)
        spot = (row // 16) * 32 + cc * 16 + row % 16
        bias_s[cc * HALF : (cc + 1) * HALF, :] = jnp.where(spot < seen, jnp.float32(0.0), low)
    row = lax.broadcasted_iota(jnp.int32, (TOK, TOK), 0)
    lane = lax.broadcasted_iota(jnp.int32, (TOK, TOK), 1)
    bias_s[2 * HALF : ROWS, :] = jnp.where(row == lane, jnp.float32(0.0), low)

    for hp in range(HEADS // 2):
        load_q(hp).wait()
        load_o(hp).wait()
        odd = qo_s[hp * TOK : (hp + 1) * TOK, :].astype(F32)
        odd = jnp.concatenate([odd[:, 64:], odd[:, :64]], axis=1)
        q_s[hp * 256 + TOK : hp * 256 + 256, :] = odd.astype(BF)
    for h in range(HEADS):
        load_g(h).wait()

    nt = (((1,), (1,)), ((), ()))

    def score(rows, at):
        s = lax.dot_general(k_s[rows, :], q_s[at, :], nt, preferred_element_type=F32)
        dp = lax.dot_general(k_s[rows, 0:HL], g_s[at, :], nt, preferred_element_type=F32)
        bias = jnp.concatenate([bias_s[rows, :], bias_s[rows, :]], axis=1)
        return s * (score_scale * log2e) + bias, dp

    def scores(rows):
        for hp in range(HEADS // 2):
            at = slice(hp * 256, hp * 256 + 256)
            s_s[rows, at], dp_s[rows, at] = score(rows, at)

    scores(slice(2 * HALF, ROWS))

    for i in range(2):
        src = core * 2 + i

        @pl.when(src != zh)
        def _():
            zg_from(src).wait_recv()

    pair = jnp.concatenate([unpack(zg_buf[core * 2 + i].astype(F32)) for i in range(2)], axis=0)
    k_s[rows16(core * HALF + xy * 16, 16), :] = pair.astype(BF)

    def xg(n):
        block = k_s.at[rows16(core * HALF + xy * 16, 16)]
        return remote(block, block, xg_send, xg_recv.at[PLANE[n][0]], at_xy(n))

    def from_x(dx):
        return k_s.at[rows16(core * HALF + ((xy // 4 + 4 - dx) % 4) * 64, 64)]

    for n in range(15):
        xg(n).start()
    for dx in (0, 1, 3, 2):
        block = from_x(dx)
        got = k_s.at[0:48] if dx == 0 else block
        remote(got, got, xg_send, xg_recv.at[dx], sib).wait_recv()
        remote(block, block, cg_send, cg_recv, sib).start()
    own_rows, other_rows = rows16(core * HALF, HALF), rows16(other * HALF, HALF)

    def keys_sent():
        most = k_s.at[0:240]
        remote(most, most, xg_send, xg_recv.at[0], sib).wait_send()
        half = k_s.at[own_rows]
        remote(half, half, cg_send, cg_recv, sib).wait_send()

    drains.append(keys_sent)

    scores(own_rows)
    half = k_s.at[other_rows]
    remote(half, half, cg_send, cg_recv, sib).wait_recv()
    rest = slice(2 * HALF, ROWS)
    for hp in range(HEADS // 2):
        at = slice(hp * 256, hp * 256 + 256)
        s, dp = zip((s_s[own_rows, at], dp_s[own_rows, at]), (s_s[rest, at], dp_s[rest, at]), score(other_rows, at))
        top = functools.reduce(jnp.maximum, [jnp.max(a, axis=0, keepdims=True) for a in s])
        e = [jnp.exp2(a - top) for a in s]
        inv = 1.0 / sum(jnp.sum(a, axis=0, keepdims=True) for a in e)
        p = [a * inv for a in e]
        delta = sum(jnp.sum(a * b, axis=0, keepdims=True) for a, b in zip(p, dp))
        for rows, a, b in zip((own_rows, rest, other_rows), p, dp):
            p_s[rows, at] = a.astype(BF)
            d_s[rows, at] = (a * (b - delta)).astype(BF)

    def key_grad(rows):
        a = jnp.dot(d_s[rows, :], q_s[...], preferred_element_type=F32) * score_scale
        b = jnp.dot(p_s[rows, :], g_s[...], preferred_element_type=F32)
        return jnp.concatenate([a[:, 0:HL] + b, a[:, HL:]], axis=1)

    kx_src[...] = key_grad(other_rows).astype(BF)
    kx = remote(kx_src, kx_buf, kx_send, kx_recv, sib)
    kx.start()
    drains.append(kx.wait_send)
    kacc[...] = key_grad(own_rows)
    ko_acc[...] = key_grad(slice(2 * HALF, ROWS))
    ko_src[...] = ko_acc[rows16(other * 64, 64), :].astype(BF)
    ko = remote(ko_src, ko_buf, ko_send, ko_recv, sib)
    ko.start()
    drains.append(ko.wait_send)
    kx.wait_recv()

    def xr(n):
        block = xr_src.at[rows16(plane(n, 1) * 16, 16)]
        return remote(block, xr_buf.at[n], xr_send, xr_recv, at_xy(n))

    for dx in (2, 1, 3, 0):
        group = rows16(((xy // 4 + dx) % 4) * 64, 64)
        xr_src[group, :] = (kacc[group, :] + kx_buf[group, :].astype(F32)).astype(BF)
        for n in range(15):
            if PLANE[n][0] == dx:
                xr(n).start()

    def oz(k):
        to = (zl + k) % 4
        return remote(os_src.at[rows16(to * 16, 16)], oz_buf.at[zl], oz_send.at[k], oz_recv.at[zl], (g, to * 2 + core))

    def oz_from(k):
        src = (zl + k) % 4
        return remote(os_src.at[0:16], oz_buf.at[src], oz_send.at[k], oz_recv.at[src], (g, src * 2 + core))

    def og(k):
        block = ow_buf.at[rows16(core * 64 + zl * 16, 16)]
        return remote(block, block, og_send.at[k], og_recv.at[zl], (g, ((zl + k) % 4) * 2 + core))

    def og_from(k):
        src = (zl + k) % 4
        block = ow_buf.at[rows16(core * 64 + src * 16, 16)]
        return remote(block, block, og_send.at[k], og_recv.at[src], (g, src * 2 + core))

    def sums_sent():
        most = xr_src.at[0:240]
        remote(most, most, xr_send, xr_recv, sib).wait_send()
        for k in range(1, 4):
            oz(k).wait_send()

    drains.append(sums_sent)

    def store_q(hp):
        return pltpu.make_async_copy(
            o_s.at[:, pl.ds(pl.multiple_of(hp * 2 * HK, 128), 2 * HK)],
            gq_hbm.at[:, pl.ds(pl.multiple_of(hp * 2 * HK, 128), 2 * HK)],
            lw.at[hp],
        )

    def query_grad(hp):
        at = pl.ds(pl.multiple_of(hp * 256, 256), 256)
        tn = (((0,), (0,)), ((), ()))
        gq = lax.dot_general(d_s[:, at], k_s[...], tn, preferred_element_type=F32) * score_scale
        even, odd = gq[0:TOK, :], gq[TOK:, :]
        odd = jnp.concatenate([odd[:, HK:], odd[:, :HK]], axis=1)
        joint = jnp.concatenate([even[:, 0:HL], even[:, HL:] + odd[:, 0:128], odd[:, 128:]], axis=1)
        o_s[:, pl.ds(pl.multiple_of(hp * 2 * HK, 128), 2 * HK)] = joint.astype(BF)
        store_q(hp).start()

    query_grad(0)
    ko.wait_recv()
    os_src[...] = (ko_acc[rows16(core * 64, 64), :] + ko_buf[...].astype(F32)).astype(BF)
    for k in range(1, 4):
        oz(k).start()
    oz_buf[zl] = os_src[rows16(zl * 16, 16), :]
    pl.loop(1, HEADS // 2)(query_grad)

    drains.append(lambda: [store_q(hp).wait() for hp in range(HEADS // 2)])
    spot = rows16(xy * 16, 16)
    total = kacc[spot, :] + kx_buf[spot, :].astype(F32)
    remote(xr_buf, xr_buf, xr_send, xr_recv, sib).wait_recv()
    for n in range(15):
        total = total + xr_buf[n].astype(F32)
    zr_src[0] = pack(total[0:8, :]).astype(BF)
    zr_src[1] = pack(total[8:16, :]).astype(BF)

    pl.semaphore_wait(relay, 1)

    def zr(i, a):
        to = (core * 2 + i) * 4 + a
        return remote(zr_src.at[i], zr_buf.at[z], zr_send, zr_recv, at_z(to))

    near = zh % 2

    @pl.when(mine)
    def _():
        for a in range(4):
            zr(1 - near, a).start()
        for k in range(1, 4):
            zr(near, (zl + k) % 4).start()

    @pl.when(jnp.logical_not(mine))
    def _():
        for a in range(4):
            zr(near, a).start()
        for a in range(4):
            zr(1 - near, a).start()

    def slabs_sent():
        @pl.when(mine)
        def _():
            remote(zr_buf.at[0:7], zr_buf.at[0:7], zr_send, zr_recv, sib).wait_send()

        @pl.when(jnp.logical_not(mine))
        def _():
            remote(zr_buf.at[0:8], zr_buf.at[0:8], zr_send, zr_recv, sib).wait_send()


    for k in range(1, 4):
        oz_from(k).wait_recv()
    own_sum = oz_buf[0].astype(F32)
    for a in range(1, 4):
        own_sum = own_sum + oz_buf[a].astype(F32)
    ow_buf[rows16(core * 64 + zl * 16, 16), :] = own_sum.astype(BF)
    for k in range(1, 4):
        og(k).start()
    drains.append(lambda: [og(k).wait_send() for k in range(1, 4)])

    for k in range(1, 4):
        og_from(k).wait_recv()
    own_half = ow_buf.at[rows16(core * 64, 64)]
    fo = remote(own_half, own_half, fo_send, fo_recv, sib)
    fo.start()
    drains.append(fo.wait_send)
    own_half = ow_buf.at[rows16(other * 64, 64)]
    remote(own_half, own_half, fo_send, fo_recv, sib).wait_recv()
    got_ref[...] = ow_buf[...].astype(F32).T[0:HK, :]
    store_go = pltpu.make_async_copy(got_ref, go_hbm, lf.at[0])
    store_go.start()
    drains.append(store_go.wait)

    for drain in drains:
        drain()

    fin = remote(fin_src, fin_buf, fin_send, fin_recv, sib)

    @pl.when(mine)
    def _():
        zr_buf[z] = zr_src[zh % 2]
        remote(zr_buf.at[0:15], zr_buf.at[0:15], zr_send, zr_recv, sib).wait_recv()
        total = jnp.zeros((16, 384), F32)
        for src in range(16):
            total = total + zr_buf[src].astype(F32)
        whole = unpack(total)
        fin_src[...] = whole
        fin.start()
        gt_ref[...] = whole[:, 0:HK]

    @pl.when(jnp.logical_not(mine))
    def _():
        fin.wait_recv()
        gt_ref[...] = fin_buf[:, 0:HK]

    store_gt = pltpu.make_async_copy(gt_ref, gt_hbm, lf.at[1])
    store_gt.start()
    slabs_sent()

    @pl.when(mine)
    def _():
        fin.wait_send()

    store_gt.wait()


def finish(q_in, t_in, o_in, q_out, t_out, o_out, q_s, t_s, o_s, sem, sem_out):
    pieces = [(q_in.at[pl.ds(i * 32, 32)], q_s.at[pl.ds(i * 32, 32)], q_out.at[pl.ds(i * 32, 32)]) for i in range(4)]
    pieces += [(o_in, o_s, o_out), (t_in, t_s, t_out)]
    loads = [pltpu.make_async_copy(p[0], p[1], sem.at[i]) for i, p in enumerate(pieces)]
    stores = [pltpu.make_async_copy(p[1], p[2], sem_out.at[i]) for i, p in enumerate(pieces)]
    for c in loads:
        c.start()
    for load, store in zip(loads, stores):
        load.wait()
        store.start()
    for c in stores:
        c.wait()


def per_device(queries, trunk, own, grad_out, visible):
    hbm = pl.BlockSpec(memory_space=pl.ANY)
    dma = pltpu.SemaphoreType.DMA
    grad_query, grad_trunk, grad_own = pl.pallas_call(
        kernel,
        out_shape=(
            jax.ShapeDtypeStruct((TOK, HEADS * HK), BF),
            jax.ShapeDtypeStruct((8, HK), F32),
            jax.ShapeDtypeStruct((HK, TOK), F32),
        ),
        in_specs=[hbm] * 5,
        out_specs=(hbm,) * 3,
        scratch_shapes=[
            pltpu.VMEM((8, HK), BF),
            pltpu.VMEM((HK, TOK), BF),
            pltpu.VMEM((TOK,), jnp.int32),
            pltpu.VMEM((8, HK), F32),
            pltpu.VMEM((HK, TOK), F32),
            pltpu.VMEM((HEADS * TOK, KP), BF),
            pltpu.VMEM((HEADS // 2 * TOK, KP), BF),
            pltpu.VMEM((HEADS * TOK, HL), BF),
            pltpu.VMEM((ROWS, KP), BF),
            pltpu.VMEM((ROWS, TOK), F32),
            pltpu.VMEM((ROWS, HEADS * TOK), F32),
            pltpu.VMEM((ROWS, HEADS * TOK), F32),
            pltpu.VMEM((ROWS, HEADS * TOK), BF),
            pltpu.VMEM((ROWS, HEADS * TOK), BF),
            pltpu.VMEM((TOK, HEADS * HK), BF),
            pltpu.VMEM((16, 384), BF),
            pltpu.VMEM((4, 16, 384), BF),
            pltpu.VMEM((HALF, KP), BF),
            pltpu.VMEM((HALF, KP), BF),
            pltpu.VMEM((HALF, KP), F32),
            pltpu.VMEM((64, KP), BF),
            pltpu.VMEM((64, KP), BF),
            pltpu.VMEM((TOK, KP), F32),
            pltpu.VMEM((HALF, KP), BF),
            pltpu.VMEM((15, 16, KP), BF),
            pltpu.VMEM((2, 16, 384), BF),
            pltpu.VMEM((16, 16, 384), BF),
            pltpu.VMEM((8, KP), F32),
            pltpu.VMEM((8, KP), F32),
            pltpu.VMEM((64, KP), BF),
            pltpu.VMEM((4, 16, KP), BF),
            pltpu.VMEM((TOK, KP), BF),
            dma((4,)), dma((4,)), dma((8,)), dma((4,)), dma((3,)), dma((2,)),
            dma((8,)), dma((4,)),
            dma, dma((4,)),
            dma, dma,
            dma, dma, dma, dma,
            dma, dma,
            dma, dma,
            dma, dma,
            dma((4,)), dma((4,)), dma((4,)), dma((4,)),
            dma, dma,
            pltpu.SemaphoreType.REGULAR,
        ],
        compiler_params=pltpu.CompilerParams(
            collective_id=0, has_side_effects=True, vmem_limit_bytes=60 * 1024 * 1024
        ),
        cost_estimate=pl.CostEstimate(flops=3860000000, bytes_accessed=4500000, transcendentals=655360),
    )(queries, trunk, own.T, grad_out, visible)
    outs = [jax.ShapeDtypeStruct(a.shape, a.dtype) for a in (grad_query, grad_trunk, grad_own)]
    grad_query, grad_trunk, grad_own = pl.pallas_call(
        finish,
        out_shape=outs,
        in_specs=[hbm] * 3,
        out_specs=[hbm] * 3,
        scratch_shapes=[pltpu.VMEM(a.shape, a.dtype) for a in outs] + [dma((6,)), dma((6,))],
        compiler_params=pltpu.CompilerParams(vmem_limit_bytes=60 * 1024 * 1024),
    )(grad_query, grad_trunk, grad_own)
    return grad_query, grad_trunk, grad_own.T


def solution(mesh):
    in_specs = (P("grp", "tp"), P("grp", None), P("grp", None), P("grp", "tp"), P("grp"))
    out_specs = (P("grp", "tp"), P("grp", None), P("grp", None))
    return jax.shard_map(
        per_device, mesh=mesh, in_specs=in_specs, out_specs=out_specs, check_vma=False
    )
```

```python
import jax
import jax.numpy as jnp
from jax import lax
from jax.experimental import pallas as pl
from jax.experimental.pallas import tpu as pltpu
from jax.sharding import PartitionSpec as P

HL = 512
HR = 64
HK = 576
KP = 640
HEADS = 8
TOK = 128
HALF = 256
ROWS = 640
MESH = pl.DeviceIdType.MESH
BF = jnp.bfloat16
F32 = jnp.float32

score_scale = 192.0 ** (-0.5)
log2e = 1.4426950408889634

PLANE = sorted(((dx, dy) for dx in range(4) for dy in range(4) if (dx, dy) != (0, 0)), key=lambda o: (-min(o[0], 4 - o[0]) - min(o[1], 4 - o[1]), o))
NEAR_Z = sorted((d for d in range(1, 16) if d < 7 or d > 9), key=lambda k: (-min(k, 16 - k), k))


def rows16(start, size):
    return pl.ds(pl.multiple_of(start, 16), size)


def remote(src, dst, send, recv, where):
    return pltpu.make_async_remote_copy(
        src_ref=src, dst_ref=dst, send_sem=send, recv_sem=recv, device_id=where, device_id_type=MESH
    )


def pack(block):
    pad = jnp.zeros((8, 128), F32)
    tail = jnp.concatenate([block[:, 384:640], pad], axis=1)
    return jnp.concatenate([block[:, 0:384], tail], axis=0)


def unpack(block):
    return jnp.concatenate([block[0:8, :], block[8:16, 0:256]], axis=1)


def kernel(
    q_hbm, tr_hbm, own_hbm, g_hbm, vis_hbm,
    gq_hbm, gt_hbm, go_hbm,
    tr_ref, own_ref, vis_ref, gt_ref, got_ref,
    q_s, qo_s, g_s, k_s, bias_s, s_s, dp_s, p_s, d_s, o_s,
    zg_src, zg_buf, kx_src, kx_buf, kacc, ko_src, ko_buf, ko_acc, xr_src, xr_buf, zr_src, zr_buf, fin_src, fin_buf,
    os_src, oz_buf, ow_buf,
    lq, lo, lg, lw, ls, lf,
    zg_send, zg_recv, xg_send, xg_recv, cg_send, cg_recv, kx_send, kx_recv, ko_send, ko_recv,
    xr_send, xr_recv, zr_send, zr_recv, fin_send, fin_recv, oz_send, oz_recv, og_send, og_recv, fo_send, fo_recv, relay,
):
    g = lax.axis_index("grp")
    t = lax.axis_index("tp")
    xy, zh = g // 4, g % 4
    zl, core = t // 2, t % 2
    z = zh * 4 + zl
    other = 1 - core
    sib = (g, zl * 2 + other)

    def plane(n, sign):
        dx, dy = PLANE[n]
        return ((xy // 4 + 4 + sign * dx) % 4) * 4 + (xy % 4 + 4 + sign * dy) % 4

    def at_xy(n):
        return (plane(n, 1) * 4 + zh, t)

    def at_z(zz):
        return (xy * 4 + zz // 4, (zz % 4) * 2 + core)

    small = [
        pltpu.make_async_copy(src, dst, ls.at[i])
        for i, (src, dst) in enumerate([(tr_hbm, tr_ref), (own_hbm, own_ref), (vis_hbm, vis_ref)])
    ]
    for copy in small:
        copy.start()

    barrier = pltpu.get_barrier_semaphore()
    for k in NEAR_Z:
        pl.semaphore_signal(barrier, inc=1, device_id=at_z((z + k) % 16), device_id_type=MESH)
    for n in range(15):
        pl.semaphore_signal(barrier, inc=1, device_id=at_xy(n), device_id_type=MESH)
    pl.semaphore_signal(barrier, inc=1, device_id=sib, device_id_type=MESH)

    def load_q(hp):
        return pltpu.make_async_copy(
            q_hbm.at[:, pl.ds(hp * 2 * HK, KP)], q_s.at[pl.ds(hp * 256, TOK)], lq.at[hp]
        )

    def load_o(hp):
        return pltpu.make_async_copy(
            q_hbm.at[:, pl.ds(hp * 2 * HK + HL, KP)], qo_s.at[pl.ds(hp * TOK, TOK)], lo.at[hp]
        )

    def load_g(h):
        return pltpu.make_async_copy(
            g_hbm.at[:, pl.ds(h * HL, HL)], g_s.at[pl.ds(h * TOK, TOK)], lg.at[h]
        )

    small[0].wait()
    slab = jnp.concatenate([tr_ref[...].astype(F32), jnp.zeros((8, KP - HK), F32)], axis=1)
    zg_src[...] = pack(slab).astype(BF)
    mine = (zh // 2) == core

    pl.semaphore_wait(barrier, 28)

    def zg(d, up):
        zz = (z + d) % 16 if up else (z + 16 - d) % 16
        return remote(zg_src, zg_buf.at[zh], zg_send.at[d], zg_recv.at[zh], at_z(zz))

    def zg_from(src):
        return remote(zg_src, zg_buf.at[src], zg_send.at[0], zg_recv.at[src], (g, t))

    for chip, up in ((3, True), (0, False)):

        @pl.when(jnp.logical_and(mine, zl == chip))
        def _():
            for d in reversed(range(1, 7)):
                zg(d, up).start()

    @pl.when(mine)
    def _():
        zg_buf[zh] = zg_src[...]

    def zg_sent():
        for chip, up in ((3, True), (0, False)):

            @pl.when(jnp.logical_and(mine, zl == chip))
            def _():
                for d in range(1, 7):
                    zg(d, up).wait_send()

    drains = [zg_sent]

    pl.semaphore_signal(relay, inc=1, device_id=at_z((z + 10) % 16), device_id_type=MESH)

    for hp in range(HEADS // 2):
        load_q(hp).start()
        load_o(hp).start()
    for h in range(HEADS):
        load_g(h).start()
    small[1].wait()
    owns = own_ref[...].astype(F32).T.astype(BF)
    k_s[2 * HALF : ROWS, :] = jnp.concatenate([owns, jnp.zeros((TOK, KP - HK), BF)], axis=1)
    small[2].wait()
    seen = vis_ref[...].reshape(1, TOK)
    low = jnp.float32(-1e30)
    for cc in range(2):
        row = lax.broadcasted_iota(jnp.int32, (HALF, TOK), 0)
        spot = (row // 16) * 32 + cc * 16 + row % 16
        bias_s[cc * HALF : (cc + 1) * HALF, :] = jnp.where(spot < seen, jnp.float32(0.0), low)
    row = lax.broadcasted_iota(jnp.int32, (TOK, TOK), 0)
    lane = lax.broadcasted_iota(jnp.int32, (TOK, TOK), 1)
    bias_s[2 * HALF : ROWS, :] = jnp.where(row == lane, jnp.float32(0.0), low)

    for hp in range(HEADS // 2):
        load_q(hp).wait()
        load_o(hp).wait()
        odd = qo_s[hp * TOK : (hp + 1) * TOK, :].astype(F32)
        odd = jnp.concatenate([odd[:, 64:], odd[:, :64]], axis=1)
        q_s[hp * 256 + TOK : hp * 256 + 256, :] = odd.astype(BF)
    for h in range(HEADS):
        load_g(h).wait()

    nt = (((1,), (1,)), ((), ()))

    def scores(rows):
        for hp in range(HEADS // 2):
            at = slice(hp * 256, hp * 256 + 256)
            s = lax.dot_general(k_s[rows, :], q_s[at, :], nt, preferred_element_type=F32)
            bias = jnp.concatenate([bias_s[rows, :], bias_s[rows, :]], axis=1)
            s_s[rows, at] = s * (score_scale * log2e) + bias
            dp_s[rows, at] = lax.dot_general(k_s[rows, 0:HL], g_s[at, :], nt, preferred_element_type=F32)

    scores(slice(2 * HALF, ROWS))

    for i in range(2):
        src = core * 2 + i

        @pl.when(src != zh)
        def _():
            zg_from(src).wait_recv()

    pair = jnp.concatenate([unpack(zg_buf[core * 2 + i].astype(F32)) for i in range(2)], axis=0)
    k_s[rows16(core * HALF + xy * 16, 16), :] = pair.astype(BF)

    def xg(k):
        block = k_s.at[rows16(core * HALF + xy * 16, 16)]
        return remote(block, block, xg_send, xg_recv.at[k], at_xy(k))

    def cg(n):
        spot = xy if n == 15 else plane(n, -1)
        block = k_s.at[rows16(core * HALF + spot * 16, 16)]
        return remote(block, block, cg_send, cg_recv, sib)

    def xg_got(n):
        block = k_s.at[rows16(core * HALF + plane(n, -1) * 16, 16)]
        return remote(block, block, xg_send, xg_recv.at[n], at_xy(n))

    for n in range(15):
        xg(n).start()
    cg(15).start()
    for n in reversed(range(15)):
        xg_got(n).wait_recv()
        cg(n).start()
    own_rows, other_rows = rows16(core * HALF, HALF), rows16(other * HALF, HALF)

    def keys_sent():
        most = k_s.at[0:240]
        remote(most, most, xg_send, xg_recv.at[0], sib).wait_send()
        half = k_s.at[own_rows]
        remote(half, half, cg_send, cg_recv, sib).wait_send()

    drains.append(keys_sent)

    scores(own_rows)
    half = k_s.at[other_rows]
    remote(half, half, cg_send, cg_recv, sib).wait_recv()
    scores(other_rows)

    for hp in range(HEADS // 2):
        at = slice(hp * 256, hp * 256 + 256)
        s, dp = s_s[:, at], dp_s[:, at]
        e = jnp.exp2(s - jnp.max(s, axis=0, keepdims=True))
        p = e * (1.0 / jnp.sum(e, axis=0, keepdims=True))
        delta = jnp.sum(p * dp, axis=0, keepdims=True)
        p_s[:, at] = p.astype(BF)
        d_s[:, at] = (p * (dp - delta)).astype(BF)

    def key_grad(rows):
        a = jnp.dot(d_s[rows, :], q_s[...], preferred_element_type=F32) * score_scale
        b = jnp.dot(p_s[rows, :], g_s[...], preferred_element_type=F32)
        return jnp.concatenate([a[:, 0:HL] + b, a[:, HL:]], axis=1)

    kx_src[...] = key_grad(other_rows).astype(BF)
    kx = remote(kx_src, kx_buf, kx_send, kx_recv, sib)
    kx.start()
    drains.append(kx.wait_send)
    kacc[...] = key_grad(own_rows)
    ko_acc[...] = key_grad(slice(2 * HALF, ROWS))
    ko_src[...] = ko_acc[rows16(other * 64, 64), :].astype(BF)
    ko = remote(ko_src, ko_buf, ko_send, ko_recv, sib)
    ko.start()
    drains.append(ko.wait_send)
    kx.wait_recv()
    total = kacc[...] + kx_buf[...].astype(F32)
    kacc[...] = total
    xr_src[...] = total.astype(BF)

    def xr(n):
        block = xr_src.at[rows16(plane(n, 1) * 16, 16)]
        return remote(block, xr_buf.at[n], xr_send, xr_recv, at_xy(n))

    for n in range(15):
        xr(n).start()

    def oz(k):
        to = (zl + k) % 4
        return remote(os_src.at[rows16(to * 16, 16)], oz_buf.at[zl], oz_send.at[k], oz_recv.at[zl], (g, to * 2 + core))

    def oz_from(k):
        src = (zl + k) % 4
        return remote(os_src.at[0:16], oz_buf.at[src], oz_send.at[k], oz_recv.at[src], (g, src * 2 + core))

    def og(k):
        block = ow_buf.at[rows16(core * 64 + zl * 16, 16)]
        return remote(block, block, og_send.at[k], og_recv.at[zl], (g, ((zl + k) % 4) * 2 + core))

    def og_from(k):
        src = (zl + k) % 4
        block = ow_buf.at[rows16(core * 64 + src * 16, 16)]
        return remote(block, block, og_send.at[k], og_recv.at[src], (g, src * 2 + core))

    def sums_sent():
        most = xr_src.at[0:240]
        remote(most, most, xr_send, xr_recv, sib).wait_send()
        for k in range(1, 4):
            oz(k).wait_send()

    drains.append(sums_sent)

    def store_q(hp):
        return pltpu.make_async_copy(
            o_s.at[:, pl.ds(pl.multiple_of(hp * 2 * HK, 128), 2 * HK)],
            gq_hbm.at[:, pl.ds(pl.multiple_of(hp * 2 * HK, 128), 2 * HK)],
            lw.at[hp],
        )

    def query_grad(hp):
        at = pl.ds(pl.multiple_of(hp * 256, 256), 256)
        tn = (((0,), (0,)), ((), ()))
        gq = lax.dot_general(d_s[:, at], k_s[...], tn, preferred_element_type=F32) * score_scale
        even, odd = gq[0:TOK, :], gq[TOK:, :]
        odd = jnp.concatenate([odd[:, HK:], odd[:, :HK]], axis=1)
        joint = jnp.concatenate([even[:, 0:HL], even[:, HL:] + odd[:, 0:128], odd[:, 128:]], axis=1)
        o_s[:, pl.ds(pl.multiple_of(hp * 2 * HK, 128), 2 * HK)] = joint.astype(BF)
        store_q(hp).start()

    query_grad(0)
    ko.wait_recv()
    os_src[...] = (ko_acc[rows16(core * 64, 64), :] + ko_buf[...].astype(F32)).astype(BF)
    for k in range(1, 4):
        oz(k).start()
    oz_buf[zl] = os_src[rows16(zl * 16, 16), :]
    pl.loop(1, HEADS // 2)(query_grad)

    drains.append(lambda: [store_q(hp).wait() for hp in range(HEADS // 2)])
    total = kacc[rows16(xy * 16, 16), :]
    remote(xr_buf, xr_buf, xr_send, xr_recv, sib).wait_recv()
    for n in range(15):
        total = total + xr_buf[n].astype(F32)
    zr_src[0] = pack(total[0:8, :]).astype(BF)
    zr_src[1] = pack(total[8:16, :]).astype(BF)

    pl.semaphore_wait(relay, 1)

    def zr(i, a):
        to = (core * 2 + i) * 4 + a
        return remote(zr_src.at[i], zr_buf.at[z], zr_send, zr_recv, at_z(to))

    for i in range(2):
        for a in range(4):

            @pl.when((core * 2 + i) * 4 + a != z)
            def _():
                zr(i, a).start()

    def slabs_sent():
        @pl.when(mine)
        def _():
            remote(zr_buf.at[0:7], zr_buf.at[0:7], zr_send, zr_recv, sib).wait_send()

        @pl.when(jnp.logical_not(mine))
        def _():
            remote(zr_buf.at[0:8], zr_buf.at[0:8], zr_send, zr_recv, sib).wait_send()


    for k in range(1, 4):
        oz_from(k).wait_recv()
    own_sum = oz_buf[0].astype(F32)
    for a in range(1, 4):
        own_sum = own_sum + oz_buf[a].astype(F32)
    ow_buf[rows16(core * 64 + zl * 16, 16), :] = own_sum.astype(BF)
    for k in range(1, 4):
        og(k).start()
    drains.append(lambda: [og(k).wait_send() for k in range(1, 4)])

    for k in range(1, 4):
        og_from(k).wait_recv()
    own_half = ow_buf.at[rows16(core * 64, 64)]
    fo = remote(own_half, own_half, fo_send, fo_recv, sib)
    fo.start()
    for drain in drains:
        drain()

    fin = remote(fin_src, fin_buf, fin_send, fin_recv, sib)

    @pl.when(mine)
    def _():
        zr_buf[z] = zr_src[zh % 2]
        remote(zr_buf.at[0:15], zr_buf.at[0:15], zr_send, zr_recv, sib).wait_recv()
        total = jnp.zeros((16, 384), F32)
        for src in range(16):
            total = total + zr_buf[src].astype(F32)
        whole = unpack(total)
        fin_src[...] = whole
        fin.start()
        gt_ref[...] = whole[:, 0:HK]

    own_half = ow_buf.at[rows16(other * 64, 64)]
    remote(own_half, own_half, fo_send, fo_recv, sib).wait_recv()
    got_ref[...] = ow_buf[...].astype(F32).T[0:HK, :]
    store_go = pltpu.make_async_copy(got_ref, go_hbm, lf.at[0])
    store_go.start()

    @pl.when(jnp.logical_not(mine))
    def _():
        fin.wait_recv()
        gt_ref[...] = fin_buf[:, 0:HK]

    store_gt = pltpu.make_async_copy(gt_ref, gt_hbm, lf.at[1])
    store_gt.start()
    slabs_sent()

    @pl.when(mine)
    def _():
        fin.wait_send()

    fo.wait_send()
    store_go.wait()
    store_gt.wait()


def finish(q_in, t_in, o_in, q_out, t_out, o_out, q_s, t_s, o_s, sem, sem_out):
    pieces = [(q_in.at[pl.ds(i * 32, 32)], q_s.at[pl.ds(i * 32, 32)], q_out.at[pl.ds(i * 32, 32)]) for i in range(4)]
    pieces += [(o_in, o_s, o_out), (t_in, t_s, t_out)]
    loads = [pltpu.make_async_copy(p[0], p[1], sem.at[i]) for i, p in enumerate(pieces)]
    stores = [pltpu.make_async_copy(p[1], p[2], sem_out.at[i]) for i, p in enumerate(pieces)]
    for c in loads:
        c.start()
    for load, store in zip(loads, stores):
        load.wait()
        store.start()
    for c in stores:
        c.wait()


def per_device(queries, trunk, own, grad_out, visible):
    hbm = pl.BlockSpec(memory_space=pl.ANY)
    dma = pltpu.SemaphoreType.DMA
    grad_query, grad_trunk, grad_own = pl.pallas_call(
        kernel,
        out_shape=(
            jax.ShapeDtypeStruct((TOK, HEADS * HK), BF),
            jax.ShapeDtypeStruct((8, HK), F32),
            jax.ShapeDtypeStruct((HK, TOK), F32),
        ),
        in_specs=[hbm] * 5,
        out_specs=(hbm,) * 3,
        scratch_shapes=[
            pltpu.VMEM((8, HK), BF),
            pltpu.VMEM((HK, TOK), BF),
            pltpu.VMEM((TOK,), jnp.int32),
            pltpu.VMEM((8, HK), F32),
            pltpu.VMEM((HK, TOK), F32),
            pltpu.VMEM((HEADS * TOK, KP), BF),
            pltpu.VMEM((HEADS // 2 * TOK, KP), BF),
            pltpu.VMEM((HEADS * TOK, HL), BF),
            pltpu.VMEM((ROWS, KP), BF),
            pltpu.VMEM((ROWS, TOK), F32),
            pltpu.VMEM((ROWS, HEADS * TOK), F32),
            pltpu.VMEM((ROWS, HEADS * TOK), F32),
            pltpu.VMEM((ROWS, HEADS * TOK), BF),
            pltpu.VMEM((ROWS, HEADS * TOK), BF),
            pltpu.VMEM((TOK, HEADS * HK), BF),
            pltpu.VMEM((16, 384), BF),
            pltpu.VMEM((4, 16, 384), BF),
            pltpu.VMEM((HALF, KP), BF),
            pltpu.VMEM((HALF, KP), BF),
            pltpu.VMEM((HALF, KP), F32),
            pltpu.VMEM((64, KP), BF),
            pltpu.VMEM((64, KP), BF),
            pltpu.VMEM((TOK, KP), F32),
            pltpu.VMEM((HALF, KP), BF),
            pltpu.VMEM((15, 16, KP), BF),
            pltpu.VMEM((2, 16, 384), BF),
            pltpu.VMEM((16, 16, 384), BF),
            pltpu.VMEM((8, KP), F32),
            pltpu.VMEM((8, KP), F32),
            pltpu.VMEM((64, KP), BF),
            pltpu.VMEM((4, 16, KP), BF),
            pltpu.VMEM((TOK, KP), BF),
            dma((4,)), dma((4,)), dma((8,)), dma((4,)), dma((3,)), dma((2,)),
            dma((8,)), dma((4,)),
            dma, dma((16,)),
            dma, dma,
            dma, dma, dma, dma,
            dma, dma,
            dma, dma,
            dma, dma,
            dma((4,)), dma((4,)), dma((4,)), dma((4,)),
            dma, dma,
            pltpu.SemaphoreType.REGULAR,
        ],
        compiler_params=pltpu.CompilerParams(
            collective_id=0, has_side_effects=True, vmem_limit_bytes=60 * 1024 * 1024
        ),
        cost_estimate=pl.CostEstimate(flops=3860000000, bytes_accessed=4500000, transcendentals=655360),
    )(queries, trunk, own.T, grad_out, visible)
    outs = [jax.ShapeDtypeStruct(a.shape, a.dtype) for a in (grad_query, grad_trunk, grad_own)]
    grad_query, grad_trunk, grad_own = pl.pallas_call(
        finish,
        out_shape=outs,
        in_specs=[hbm] * 3,
        out_specs=[hbm] * 3,
        scratch_shapes=[pltpu.VMEM(a.shape, a.dtype) for a in outs] + [dma((6,)), dma((6,))],
        compiler_params=pltpu.CompilerParams(vmem_limit_bytes=60 * 1024 * 1024),
    )(grad_query, grad_trunk, grad_own)
    return grad_query, grad_trunk, grad_own.T


def solution(mesh):
    in_specs = (P("grp", "tp"), P("grp", None), P("grp", None), P("grp", "tp"), P("grp"))
    out_specs = (P("grp", "tp"), P("grp", None), P("grp", None))
    return jax.shard_map(
        per_device, mesh=mesh, in_specs=in_specs, out_specs=out_specs, check_vma=False
    )
```

```python
import jax
import jax.numpy as jnp
from jax import lax
from jax.experimental import pallas as pl
from jax.experimental.pallas import tpu as pltpu
from jax.sharding import PartitionSpec as P

HL = 512
HR = 64
HK = 576
KP = 640
HEADS = 8
TOK = 128
HALF = 256
ROWS = 640
MESH = pl.DeviceIdType.MESH
BF = jnp.bfloat16
F32 = jnp.float32

score_scale = 192.0 ** (-0.5)
log2e = 1.4426950408889634

PLANE = sorted(((dx, dy) for dx in range(4) for dy in range(4) if (dx, dy) != (0, 0)), key=lambda o: (-min(o[0], 4 - o[0]) - min(o[1], 4 - o[1]), o))
NEAR_Z = sorted((d for d in range(1, 16) if d < 7 or d > 9), key=lambda k: (-min(k, 16 - k), k))


def rows16(start, size):
    return pl.ds(pl.multiple_of(start, 16), size)


def remote(src, dst, send, recv, where):
    return pltpu.make_async_remote_copy(
        src_ref=src, dst_ref=dst, send_sem=send, recv_sem=recv, device_id=where, device_id_type=MESH
    )


def pack(block):
    pad = jnp.zeros((8, 128), F32)
    tail = jnp.concatenate([block[:, 384:640], pad], axis=1)
    return jnp.concatenate([block[:, 0:384], tail], axis=0)


def unpack(block):
    return jnp.concatenate([block[0:8, :], block[8:16, 0:256]], axis=1)


def kernel(
    q_hbm, tr_hbm, own_hbm, g_hbm, vis_hbm,
    gq_hbm, gt_hbm, go_hbm,
    tr_ref, own_ref, vis_ref, gt_ref, got_ref,
    q_s, qo_s, g_s, k_s, bias_s, s_s, dp_s, p_s, d_s, o_s,
    zg_src, zg_buf, kx_src, kx_buf, kacc, ko_src, ko_buf, ko_acc, xr_src, xr_buf, zr_src, zr_buf, fin_src, fin_buf,
    os_src, oz_buf, ow_buf,
    lq, lo, lg, lw, ls, lf,
    zg_send, zg_recv, xg_send, xg_recv, cg_send, cg_recv, kx_send, kx_recv, ko_send, ko_recv,
    xr_send, xr_recv, zr_send, zr_recv, fin_send, fin_recv, oz_send, oz_recv, og_send, og_recv, fo_send, fo_recv, relay,
):
    g = lax.axis_index("grp")
    t = lax.axis_index("tp")
    xy, zh = g // 4, g % 4
    zl, core = t // 2, t % 2
    z = zh * 4 + zl
    other = 1 - core
    sib = (g, zl * 2 + other)

    def plane(n, sign):
        dx, dy = PLANE[n]
        return ((xy // 4 + 4 + sign * dx) % 4) * 4 + (xy % 4 + 4 + sign * dy) % 4

    def at_xy(n):
        return (plane(n, 1) * 4 + zh, t)

    def at_z(zz):
        return (xy * 4 + zz // 4, (zz % 4) * 2 + core)

    small = [
        pltpu.make_async_copy(src, dst, ls.at[i])
        for i, (src, dst) in enumerate([(tr_hbm, tr_ref), (own_hbm, own_ref), (vis_hbm, vis_ref)])
    ]
    for copy in small:
        copy.start()

    barrier = pltpu.get_barrier_semaphore()
    for k in NEAR_Z:
        pl.semaphore_signal(barrier, inc=1, device_id=at_z((z + k) % 16), device_id_type=MESH)
    for n in range(15):
        pl.semaphore_signal(barrier, inc=1, device_id=at_xy(n), device_id_type=MESH)
    pl.semaphore_signal(barrier, inc=1, device_id=sib, device_id_type=MESH)

    def load_q(hp):
        return pltpu.make_async_copy(
            q_hbm.at[:, pl.ds(hp * 2 * HK, KP)], q_s.at[pl.ds(hp * 256, TOK)], lq.at[hp]
        )

    def load_o(hp):
        return pltpu.make_async_copy(
            q_hbm.at[:, pl.ds(hp * 2 * HK + HL, KP)], qo_s.at[pl.ds(hp * TOK, TOK)], lo.at[hp]
        )

    def load_g(h):
        return pltpu.make_async_copy(
            g_hbm.at[:, pl.ds(h * HL, HL)], g_s.at[pl.ds(h * TOK, TOK)], lg.at[h]
        )

    small[0].wait()
    slab = jnp.concatenate([tr_ref[...].astype(F32), jnp.zeros((8, KP - HK), F32)], axis=1)
    zg_src[...] = pack(slab).astype(BF)
    for hp in range(HEADS // 2):
        load_q(hp).start()
        load_o(hp).start()
    for h in range(HEADS):
        load_g(h).start()
    mine = (zh // 2) == core

    pl.semaphore_wait(barrier, 28)

    def zg(d, up):
        zz = (z + d) % 16 if up else (z + 16 - d) % 16
        return remote(zg_src, zg_buf.at[zh], zg_send.at[d], zg_recv.at[zh], at_z(zz))

    def zg_from(src):
        return remote(zg_src, zg_buf.at[src], zg_send.at[0], zg_recv.at[src], (g, t))

    for chip, up in ((3, True), (0, False)):

        @pl.when(jnp.logical_and(mine, zl == chip))
        def _():
            for d in reversed(range(1, 7)):
                zg(d, up).start()

    @pl.when(mine)
    def _():
        zg_buf[zh] = zg_src[...]

    def zg_sent():
        for chip, up in ((3, True), (0, False)):

            @pl.when(jnp.logical_and(mine, zl == chip))
            def _():
                for d in range(1, 7):
                    zg(d, up).wait_send()

    drains = [zg_sent]

    pl.semaphore_signal(relay, inc=1, device_id=at_z((z + 10) % 16), device_id_type=MESH)

    small[1].wait()
    owns = own_ref[...].astype(F32).T.astype(BF)
    k_s[2 * HALF : ROWS, :] = jnp.concatenate([owns, jnp.zeros((TOK, KP - HK), BF)], axis=1)
    small[2].wait()
    seen = vis_ref[...].reshape(1, TOK)
    low = jnp.float32(-1e30)
    for cc in range(2):
        row = lax.broadcasted_iota(jnp.int32, (HALF, TOK), 0)
        spot = (row // 16) * 32 + cc * 16 + row % 16
        bias_s[cc * HALF : (cc + 1) * HALF, :] = jnp.where(spot < seen, jnp.float32(0.0), low)
    row = lax.broadcasted_iota(jnp.int32, (TOK, TOK), 0)
    lane = lax.broadcasted_iota(jnp.int32, (TOK, TOK), 1)
    bias_s[2 * HALF : ROWS, :] = jnp.where(row == lane, jnp.float32(0.0), low)

    for hp in range(HEADS // 2):
        load_q(hp).wait()
        load_o(hp).wait()
        odd = qo_s[hp * TOK : (hp + 1) * TOK, :].astype(F32)
        odd = jnp.concatenate([odd[:, 64:], odd[:, :64]], axis=1)
        q_s[hp * 256 + TOK : hp * 256 + 256, :] = odd.astype(BF)
    for h in range(HEADS):
        load_g(h).wait()

    nt = (((1,), (1,)), ((), ()))

    def scores(rows):
        for hp in range(HEADS // 2):
            at = slice(hp * 256, hp * 256 + 256)
            s = lax.dot_general(k_s[rows, :], q_s[at, :], nt, preferred_element_type=F32)
            bias = jnp.concatenate([bias_s[rows, :], bias_s[rows, :]], axis=1)
            s_s[rows, at] = s * (score_scale * log2e) + bias
            dp_s[rows, at] = lax.dot_general(k_s[rows, 0:HL], g_s[at, :], nt, preferred_element_type=F32)

    scores(slice(2 * HALF, ROWS))

    for i in range(2):
        src = core * 2 + i

        @pl.when(src != zh)
        def _():
            zg_from(src).wait_recv()

    pair = jnp.concatenate([unpack(zg_buf[core * 2 + i].astype(F32)) for i in range(2)], axis=0)
    k_s[rows16(core * HALF + xy * 16, 16), :] = pair.astype(BF)

    def xg(k):
        block = k_s.at[rows16(core * HALF + xy * 16, 16)]
        return remote(block, block, xg_send, xg_recv.at[k], at_xy(k))

    def cg(n):
        spot = xy if n == 15 else plane(n, -1)
        block = k_s.at[rows16(core * HALF + spot * 16, 16)]
        return remote(block, block, cg_send, cg_recv, sib)

    def xg_got(n):
        block = k_s.at[rows16(core * HALF + plane(n, -1) * 16, 16)]
        return remote(block, block, xg_send, xg_recv.at[n], at_xy(n))

    for n in range(15):
        xg(n).start()
    cg(15).start()
    for n in reversed(range(15)):
        xg_got(n).wait_recv()
        cg(n).start()
    own_rows, other_rows = rows16(core * HALF, HALF), rows16(other * HALF, HALF)

    def keys_sent():
        most = k_s.at[0:240]
        remote(most, most, xg_send, xg_recv.at[0], sib).wait_send()
        half = k_s.at[own_rows]
        remote(half, half, cg_send, cg_recv, sib).wait_send()

    drains.append(keys_sent)

    scores(own_rows)
    half = k_s.at[other_rows]
    remote(half, half, cg_send, cg_recv, sib).wait_recv()
    scores(other_rows)

    for hp in range(HEADS // 2):
        at = slice(hp * 256, hp * 256 + 256)
        s, dp = s_s[:, at], dp_s[:, at]
        e = jnp.exp2(s - jnp.max(s, axis=0, keepdims=True))
        p = e * (1.0 / jnp.sum(e, axis=0, keepdims=True))
        delta = jnp.sum(p * dp, axis=0, keepdims=True)
        p_s[:, at] = p.astype(BF)
        d_s[:, at] = (p * (dp - delta)).astype(BF)

    def key_grad(rows):
        a = jnp.dot(d_s[rows, :], q_s[...], preferred_element_type=F32) * score_scale
        b = jnp.dot(p_s[rows, :], g_s[...], preferred_element_type=F32)
        return jnp.concatenate([a[:, 0:HL] + b, a[:, HL:]], axis=1)

    kx_src[...] = key_grad(other_rows).astype(BF)
    kx = remote(kx_src, kx_buf, kx_send, kx_recv, sib)
    kx.start()
    drains.append(kx.wait_send)
    kacc[...] = key_grad(own_rows)
    ko_acc[...] = key_grad(slice(2 * HALF, ROWS))
    ko_src[...] = ko_acc[rows16(other * 64, 64), :].astype(BF)
    ko = remote(ko_src, ko_buf, ko_send, ko_recv, sib)
    ko.start()
    drains.append(ko.wait_send)
    kx.wait_recv()
    total = kacc[...] + kx_buf[...].astype(F32)
    kacc[...] = total
    xr_src[...] = total.astype(BF)

    def xr(n):
        block = xr_src.at[rows16(plane(n, 1) * 16, 16)]
        return remote(block, xr_buf.at[n], xr_send, xr_recv, at_xy(n))

    for n in range(15):
        xr(n).start()

    def oz(k):
        to = (zl + k) % 4
        return remote(os_src.at[rows16(to * 16, 16)], oz_buf.at[zl], oz_send.at[k], oz_recv.at[zl], (g, to * 2 + core))

    def oz_from(k):
        src = (zl + k) % 4
        return remote(os_src.at[0:16], oz_buf.at[src], oz_send.at[k], oz_recv.at[src], (g, src * 2 + core))

    def og(k):
        block = ow_buf.at[rows16(core * 64 + zl * 16, 16)]
        return remote(block, block, og_send.at[k], og_recv.at[zl], (g, ((zl + k) % 4) * 2 + core))

    def og_from(k):
        src = (zl + k) % 4
        block = ow_buf.at[rows16(core * 64 + src * 16, 16)]
        return remote(block, block, og_send.at[k], og_recv.at[src], (g, src * 2 + core))

    def sums_sent():
        most = xr_src.at[0:240]
        remote(most, most, xr_send, xr_recv, sib).wait_send()
        for k in range(1, 4):
            oz(k).wait_send()

    drains.append(sums_sent)

    def store_q(hp):
        return pltpu.make_async_copy(
            o_s.at[:, pl.ds(pl.multiple_of(hp * 2 * HK, 128), 2 * HK)],
            gq_hbm.at[:, pl.ds(pl.multiple_of(hp * 2 * HK, 128), 2 * HK)],
            lw.at[hp],
        )

    def query_grad(hp):
        at = pl.ds(pl.multiple_of(hp * 256, 256), 256)
        tn = (((0,), (0,)), ((), ()))
        gq = lax.dot_general(d_s[:, at], k_s[...], tn, preferred_element_type=F32) * score_scale
        even, odd = gq[0:TOK, :], gq[TOK:, :]
        odd = jnp.concatenate([odd[:, HK:], odd[:, :HK]], axis=1)
        joint = jnp.concatenate([even[:, 0:HL], even[:, HL:] + odd[:, 0:128], odd[:, 128:]], axis=1)
        o_s[:, pl.ds(pl.multiple_of(hp * 2 * HK, 128), 2 * HK)] = joint.astype(BF)
        store_q(hp).start()

    query_grad(0)
    ko.wait_recv()
    os_src[...] = (ko_acc[rows16(core * 64, 64), :] + ko_buf[...].astype(F32)).astype(BF)
    for k in range(1, 4):
        oz(k).start()
    oz_buf[zl] = os_src[rows16(zl * 16, 16), :]
    pl.loop(1, HEADS // 2)(query_grad)

    drains.append(lambda: [store_q(hp).wait() for hp in range(HEADS // 2)])
    total = kacc[rows16(xy * 16, 16), :]
    remote(xr_buf, xr_buf, xr_send, xr_recv, sib).wait_recv()
    for n in range(15):
        total = total + xr_buf[n].astype(F32)
    zr_src[0] = pack(total[0:8, :]).astype(BF)
    zr_src[1] = pack(total[8:16, :]).astype(BF)

    pl.semaphore_wait(relay, 1)

    def zr(i, a):
        to = (core * 2 + i) * 4 + a
        return remote(zr_src.at[i], zr_buf.at[z], zr_send, zr_recv, at_z(to))

    for i in range(2):
        for a in range(4):

            @pl.when((core * 2 + i) * 4 + a != z)
            def _():
                zr(i, a).start()

    def slabs_sent():
        @pl.when(mine)
        def _():
            remote(zr_buf.at[0:7], zr_buf.at[0:7], zr_send, zr_recv, sib).wait_send()

        @pl.when(jnp.logical_not(mine))
        def _():
            remote(zr_buf.at[0:8], zr_buf.at[0:8], zr_send, zr_recv, sib).wait_send()


    for k in range(1, 4):
        oz_from(k).wait_recv()
    own_sum = oz_buf[0].astype(F32)
    for a in range(1, 4):
        own_sum = own_sum + oz_buf[a].astype(F32)
    ow_buf[rows16(core * 64 + zl * 16, 16), :] = own_sum.astype(BF)
    for k in range(1, 4):
        og(k).start()
    drains.append(lambda: [og(k).wait_send() for k in range(1, 4)])

    for k in range(1, 4):
        og_from(k).wait_recv()
    own_half = ow_buf.at[rows16(core * 64, 64)]
    fo = remote(own_half, own_half, fo_send, fo_recv, sib)
    fo.start()
    for drain in drains:
        drain()

    fin = remote(fin_src, fin_buf, fin_send, fin_recv, sib)

    @pl.when(mine)
    def _():
        zr_buf[z] = zr_src[zh % 2]
        remote(zr_buf.at[0:15], zr_buf.at[0:15], zr_send, zr_recv, sib).wait_recv()
        total = jnp.zeros((16, 384), F32)
        for src in range(16):
            total = total + zr_buf[src].astype(F32)
        whole = unpack(total)
        fin_src[...] = whole
        fin.start()
        gt_ref[...] = whole[:, 0:HK]

    own_half = ow_buf.at[rows16(other * 64, 64)]
    remote(own_half, own_half, fo_send, fo_recv, sib).wait_recv()
    got_ref[...] = ow_buf[...].astype(F32).T[0:HK, :]
    store_go = pltpu.make_async_copy(got_ref, go_hbm, lf.at[0])
    store_go.start()

    @pl.when(jnp.logical_not(mine))
    def _():
        fin.wait_recv()
        gt_ref[...] = fin_buf[:, 0:HK]

    store_gt = pltpu.make_async_copy(gt_ref, gt_hbm, lf.at[1])
    store_gt.start()
    slabs_sent()

    @pl.when(mine)
    def _():
        fin.wait_send()

    fo.wait_send()
    store_go.wait()
    store_gt.wait()


def finish(q_in, t_in, o_in, q_out, t_out, o_out, q_s, t_s, o_s, sem, sem_out):
    pieces = [(q_in.at[pl.ds(i * 32, 32)], q_s.at[pl.ds(i * 32, 32)], q_out.at[pl.ds(i * 32, 32)]) for i in range(4)]
    pieces += [(o_in, o_s, o_out), (t_in, t_s, t_out)]
    loads = [pltpu.make_async_copy(p[0], p[1], sem.at[i]) for i, p in enumerate(pieces)]
    stores = [pltpu.make_async_copy(p[1], p[2], sem_out.at[i]) for i, p in enumerate(pieces)]
    for c in loads:
        c.start()
    for load, store in zip(loads, stores):
        load.wait()
        store.start()
    for c in stores:
        c.wait()


def per_device(queries, trunk, own, grad_out, visible):
    hbm = pl.BlockSpec(memory_space=pl.ANY)
    dma = pltpu.SemaphoreType.DMA
    grad_query, grad_trunk, grad_own = pl.pallas_call(
        kernel,
        out_shape=(
            jax.ShapeDtypeStruct((TOK, HEADS * HK), BF),
            jax.ShapeDtypeStruct((8, HK), F32),
            jax.ShapeDtypeStruct((HK, TOK), F32),
        ),
        in_specs=[hbm] * 5,
        out_specs=(hbm,) * 3,
        scratch_shapes=[
            pltpu.VMEM((8, HK), BF),
            pltpu.VMEM((HK, TOK), BF),
            pltpu.VMEM((TOK,), jnp.int32),
            pltpu.VMEM((8, HK), F32),
            pltpu.VMEM((HK, TOK), F32),
            pltpu.VMEM((HEADS * TOK, KP), BF),
            pltpu.VMEM((HEADS // 2 * TOK, KP), BF),
            pltpu.VMEM((HEADS * TOK, HL), BF),
            pltpu.VMEM((ROWS, KP), BF),
            pltpu.VMEM((ROWS, TOK), F32),
            pltpu.VMEM((ROWS, HEADS * TOK), F32),
            pltpu.VMEM((ROWS, HEADS * TOK), F32),
            pltpu.VMEM((ROWS, HEADS * TOK), BF),
            pltpu.VMEM((ROWS, HEADS * TOK), BF),
            pltpu.VMEM((TOK, HEADS * HK), BF),
            pltpu.VMEM((16, 384), BF),
            pltpu.VMEM((4, 16, 384), BF),
            pltpu.VMEM((HALF, KP), BF),
            pltpu.VMEM((HALF, KP), BF),
            pltpu.VMEM((HALF, KP), F32),
            pltpu.VMEM((64, KP), BF),
            pltpu.VMEM((64, KP), BF),
            pltpu.VMEM((TOK, KP), F32),
            pltpu.VMEM((HALF, KP), BF),
            pltpu.VMEM((15, 16, KP), BF),
            pltpu.VMEM((2, 16, 384), BF),
            pltpu.VMEM((16, 16, 384), BF),
            pltpu.VMEM((8, KP), F32),
            pltpu.VMEM((8, KP), F32),
            pltpu.VMEM((64, KP), BF),
            pltpu.VMEM((4, 16, KP), BF),
            pltpu.VMEM((TOK, KP), BF),
            dma((4,)), dma((4,)), dma((8,)), dma((4,)), dma((3,)), dma((2,)),
            dma((8,)), dma((4,)),
            dma, dma((16,)),
            dma, dma,
            dma, dma, dma, dma,
            dma, dma,
            dma, dma,
            dma, dma,
            dma((4,)), dma((4,)), dma((4,)), dma((4,)),
            dma, dma,
            pltpu.SemaphoreType.REGULAR,
        ],
        compiler_params=pltpu.CompilerParams(
            collective_id=0, has_side_effects=True, vmem_limit_bytes=60 * 1024 * 1024
        ),
        cost_estimate=pl.CostEstimate(flops=3860000000, bytes_accessed=4500000, transcendentals=655360),
    )(queries, trunk, own.T, grad_out, visible)
    outs = [jax.ShapeDtypeStruct(a.shape, a.dtype) for a in (grad_query, grad_trunk, grad_own)]
    grad_query, grad_trunk, grad_own = pl.pallas_call(
        finish,
        out_shape=outs,
        in_specs=[hbm] * 3,
        out_specs=[hbm] * 3,
        scratch_shapes=[pltpu.VMEM(a.shape, a.dtype) for a in outs] + [dma((6,)), dma((6,))],
        compiler_params=pltpu.CompilerParams(vmem_limit_bytes=60 * 1024 * 1024),
    )(grad_query, grad_trunk, grad_own)
    return grad_query, grad_trunk, grad_own.T


def solution(mesh):
    in_specs = (P("grp", "tp"), P("grp", None), P("grp", None), P("grp", "tp"), P("grp"))
    out_specs = (P("grp", "tp"), P("grp", None), P("grp", None))
    return jax.shard_map(
        per_device, mesh=mesh, in_specs=in_specs, out_specs=out_specs, check_vma=False
    )
```
